32 devices in a mesh: dp: 8 (over y, x, core), seq: 4 (over z).
Axes of the slice: x: 2, y: 2, z: 4, core: 2. Of those that a mesh axis runs over, the one named last changes fastest.
Arguments:
- tokens: bfloat16 [8, 1024, 768], P('dp', 'seq'), may hold values from -6 to 6
- codon_positions: int32 [8, 1024], P('dp', 'seq'), may hold values from 0 to 4093, as said below
- start_flags: int32 [8], P('dp'), may hold values 0 or 1
- start_embed: float32 [768], replicated, may hold values from -3 to 3
- norm_gain: float32 [2, 768], replicated, may hold values from 0.25 to 1.75
- norm_shift: float32 [2, 768], replicated, may hold values from -2 to 2
- w_qkv: bfloat16 [768, 2304], replicated, may hold values from -0.21875 to 0.21875
- b_qkv: float32 [2304], replicated, may hold values from -3 to 3
- w_out: bfloat16 [768, 768], replicated, may hold values from -0.875 to 0.875
- b_out: float32 [768], replicated, may hold values from -3 to 3
- w_up: bfloat16 [768, 3072], replicated, may hold values from -0.21875 to 0.21875
- b_up: float32 [3072], replicated, may hold values from -3 to 3
- w_down: bfloat16 [3072, 768], replicated, may hold values from -0.21875 to 0.21875
- b_down: float32 [768], replicated, may hold values from -3 to 3
- cotangent: bfloat16 [8, 1024, 768], P('dp', 'seq'), may hold values from -6 to 6
Outputs:
- layer_out: bfloat16 [8, 1024, 768], P('dp', 'seq')
- grad_tokens: bfloat16 [8, 1024, 768], P('dp', 'seq')
- grad_start: float32 [768], replicated
- grad_gain: float32 [2, 768], replicated
- grad_shift: float32 [2, 768], replicated
- grad_w_qkv: float32 [768, 2304], replicated
- grad_b_qkv: float32 [2304], replicated
- grad_w_out: float32 [768, 768], replicated
- grad_b_out: float32 [768], replicated
- grad_w_up: float32 [768, 3072], replicated
- grad_b_up: float32 [3072], replicated
- grad_w_down: float32 [3072, 768], replicated
- grad_b_down: float32 [768], replicated
The draws below stay inside these ranges and needn't reach their ends.
Inputs may be any that keep to these rules, and one draw needn't show every extreme that they name: `codon_positions`: within a gene the position rises by 1 or 2 from one codon to the next; some gene starts at 0, and some gene ends at the largest position.
All inputs are finite; a program needn't handle non-finite values. No bound on the sum of `start_flags` on one device may be relied on, other than what follows from the above.
Results may differ from the reference program's by a relative error of at most 0.013.
Values may be sent and summed in bfloat16 or wider, within the bound.
No kernel may reach another device: no remote copies, remote signals or barrier semaphores. Data moves between devices by JAX's collectives and lax.ppermute only.
A program may use at most 192 MiB of HBM per device.

```python
import jax
import jax.numpy as jnp
from jax import lax

D = 768
HEADS = 12
HEAD_DIM = 64
FF = 3072
L = 1024
SEQS = 8


def draw_codon_positions(key, part):
    offset_key = jax.random.fold_in(key, 11)
    stride_key = jax.random.fold_in(key, 12)
    offsets = jax.random.randint(offset_key, (SEQS, 1), 0, 2048)
    offsets = offsets.at[0, 0].set(0).at[SEQS - 1, 0].set(2047)
    strides = jax.random.randint(stride_key, (SEQS, L), 1, 3)
    strides = strides.at[SEQS - 1].set(2)
    return (offsets + jnp.cumsum(strides, axis=1) - strides).astype(jnp.int32)


def with_ends(drawn, stream_key, smallest, high):
    dims = drawn.shape
    index_at = [jax.random.randint(jax.random.fold_in(stream_key, axis), (), 0, dims[axis]) for axis in range(len(dims))]
    drawn = drawn.at[tuple(index_at)].set(smallest)
    longest = dims.index(max(dims))
    index_at[longest] = (index_at[longest] + 1) % dims[longest]
    return drawn.at[tuple(index_at)].set(high)


def levels(stream_key, extent, cuts, low, top_value):
    gain, own = 1.0, jax.random.fold_in(stream_key, 6)
    for axis_at, blocks in cuts:
        steps = jnp.exp(jax.random.uniform(jax.random.fold_in(own, axis_at), (blocks,), jnp.float32, low / len(cuts), top_value / len(cuts)))
        gain = gain * jnp.repeat(steps, extent[axis_at] // blocks).reshape([-1 if axis == axis_at else 1 for axis in range(len(extent))])
    return gain


def normal_values(rng, shape, deviation, limit, shards=(), kind=jnp.bfloat16):
    drawn = jax.random.normal(rng, shape, jnp.float32) * deviation
    if len(shards) > 0:
        drawn = levels(rng, shape, shards, -0.22, 0.18) * drawn
    return jnp.clip(drawn, min=-limit, max=limit).astype(kind)


def setup_inputs(seed: int = 0) -> dict:
    arg_keys = jax.random.split(jax.random.key(seed), 16)
    return {
        "tokens": normal_values(arg_keys[0], (SEQS, L, D), 1.0, 6.0, ((0, 8), (1, 4))),
        "codon_positions": draw_codon_positions(jax.random.fold_in(arg_keys[15], 71), 0),
        "start_flags": with_ends((jax.random.randint(arg_keys[2], (SEQS,), 0, 2) < 1).astype(jnp.int32), jax.random.fold_in(arg_keys[2], 1), 0, 1),
        "start_embed": normal_values(arg_keys[3], (D,), 0.5, 3.0, (), jnp.float32),
        "norm_gain": jnp.clip(1.0 + 0.15 * jax.random.normal(arg_keys[4], (2, D), jnp.float32), 0.25, 1.75),
        "norm_shift": normal_values(arg_keys[5], (2, D), 0.3, 2.0, (), jnp.float32),
        "w_qkv": normal_values(arg_keys[6], (D, 3 * D), D ** -0.5, 0.21875),
        "b_qkv": normal_values(arg_keys[7], (3 * D,), 0.5, 3.0, (), jnp.float32),
        "w_out": normal_values(arg_keys[8], (D, D), (D // 16) ** -0.5, 0.875),
        "b_out": normal_values(arg_keys[9], (D,), 0.5, 3.0, (), jnp.float32),
        "w_up": normal_values(arg_keys[10], (D, FF), D ** -0.5, 0.21875),
        "b_up": normal_values(arg_keys[11], (FF,), 0.5, 3.0, (), jnp.float32),
        "w_down": normal_values(arg_keys[12], (FF, D), (FF // 4) ** -0.5, 0.21875),
        "b_down": normal_values(arg_keys[13], (D,), 0.5, 3.0, (), jnp.float32),
        "cotangent": normal_values(arg_keys[14], (SEQS, L, D), 1.0, 6.0, ((0, 8), (1, 4))),
    }


highest = lax.Precision.HIGHEST
epsilon = 1e-05

@jax.custom_vjp
def low(v):
    return lax.optimization_barrier(v.astype(jnp.bfloat16)).astype(jnp.float32)

@jax.custom_vjp
def low_back(v):
    return v

def low_keep(v):
    return (low(v), None)

def low_pass(kept, grad):
    return (grad,)

def back_keep(v):
    return (v, None)

def back_low(kept, grad):
    return (low(grad),)
low.defvjp(low_keep, low_pass)
low_back.defvjp(back_keep, back_low)

def normalize(values, gain_row, shift_row):
    centered = values - lax.optimization_barrier(jnp.mean(values, axis=-1, keepdims=True))
    inverse = lax.rsqrt(lax.optimization_barrier(jnp.mean(centered * centered, axis=-1, keepdims=True)) + epsilon)
    return centered * inverse * gain_row + shift_row

def rotate(values, cos_table, sin_table):
    middle_index = values.shape[-1] // 2
    former = values[..., :middle_index]
    latter = values[..., middle_index:]
    return jnp.concatenate([former * cos_table - latter * sin_table, latter * cos_table + former * sin_table], axis=-1)

def encoder_layer(params, inputs, cos_table, sin_table, flag_values):
    start_embed, norm_gain, norm_shift, w_qkv, b_qkv, w_out, b_out, w_up, b_up, w_down, b_down = params
    batch_size, length, model_width = inputs.shape
    residual = inputs + flag_values[:, None, None] * start_embed
    normed = low(normalize(residual, norm_gain[0], norm_shift[0]))
    mixed_proj = jnp.einsum('bld,de->ble', normed, w_qkv, precision=highest) + b_qkv
    mixed_proj = low_back(mixed_proj).reshape(batch_size, length, HEADS, 3, HEAD_DIM)
    queries = low(low_back(rotate(mixed_proj[:, :, :, 0], cos_table, sin_table)))
    keyset = low(low_back(rotate(mixed_proj[:, :, :, 1], cos_table, sin_table)))
    valueset = low(mixed_proj[:, :, :, 2])
    block_rows = min(512, length)
    factor = HEAD_DIM ** (-0.5)

    def attend(query_block):
        scores = low_back(jnp.einsum('bqhe,bkhe->bhqk', query_block, keyset, precision=highest) * factor)
        weights = low(jax.nn.softmax(scores, axis=-1))
        return jnp.einsum('bhqk,bkhe->bqhe', weights, valueset, precision=highest)
    blocked = jnp.moveaxis(queries.reshape(batch_size, length // block_rows, block_rows, HEADS, HEAD_DIM), 1, 0)
    attended = jnp.moveaxis(lax.map(jax.checkpoint(attend), blocked), 0, 1).reshape(batch_size, length, model_width)
    attended = low(low_back(attended))
    branch = low_back(jnp.einsum('bld,de->ble', attended, w_out, precision=highest) + b_out)
    middle = residual + branch
    second = low(normalize(middle, norm_gain[1], norm_shift[1]))
    hidden = low_back(jnp.einsum('bld,df->blf', second, w_up, precision=highest) + b_up)
    active = low(jax.nn.gelu(hidden, approximate=False))
    return middle + jnp.einsum('blf,fd->bld', active, w_down, precision=highest) + b_down

def reference(tokens, codon_positions, start_flags, start_embed, norm_gain, norm_shift, w_qkv, b_qkv, w_out, b_out, w_up, b_up, w_down, b_down, cotangent):
    params = (start_embed, norm_gain, norm_shift, w_qkv.astype(jnp.float32), b_qkv, w_out.astype(jnp.float32), b_out, w_up.astype(jnp.float32), b_up, w_down.astype(jnp.float32), b_down)
    group_size = max((divisor for divisor in range(1, SEQS + 1) if SEQS % divisor == 0 and divisor * L <= 4096))
    rounds = SEQS // group_size
    half_dim = HEAD_DIM // 2
    frequency = 10000.0 ** (-2.0 * jnp.arange(half_dim, dtype=jnp.float32) / HEAD_DIM)
    angles = codon_positions.astype(jnp.float32)[:, :, None, None] * frequency
    cos_table = jnp.cos(angles)
    sin_table = jnp.sin(angles)

    def regroup(array):
        return array.reshape((rounds, group_size) + array.shape[1:])
    inputs = (regroup(tokens.astype(jnp.float32)), regroup(cos_table), regroup(sin_table), regroup(start_flags.astype(jnp.float32)), regroup(cotangent.astype(jnp.float32)))

    def advance(totals, pieces):
        token_block, cos_block, sin_block, flag_block, cot_block = pieces
        result, pullback = jax.vjp(lambda weights, rows: encoder_layer(weights, rows, cos_block, sin_block, flag_block), params, token_block)
        gradients, grad_rows = pullback(cot_block)
        return (jax.tree.map(jnp.add, totals, gradients), (result.astype(jnp.bfloat16), grad_rows.astype(jnp.bfloat16)))
    totals, (outputs, grad_inputs) = lax.scan(advance, jax.tree.map(jnp.zeros_like, params), inputs)
    grad_start, grad_gain, grad_shift, grad_qkv, grad_bqkv, grad_wout, grad_bout, grad_up, grad_bup, grad_down, grad_bdown = totals
    return (outputs.reshape(tokens.shape), grad_inputs.reshape(tokens.shape), grad_start, grad_gain, grad_shift, grad_qkv, grad_bqkv, grad_wout, grad_bout, grad_up, grad_bup, grad_down, grad_bdown)
```

```python
import math

import jax
import jax.numpy as jnp
from jax import lax
from jax.experimental import pallas as pl
from jax.experimental.pallas import tpu as pltpu
from jax.sharding import PartitionSpec as P

HEADS = 12
HEAD_DIM = 64
EPS = 1e-05
BF = jnp.bfloat16
F32 = jnp.float32
VMEM_LIMIT = 56 * 1024 * 1024
HEADS_PER_STEP = 4


def dot(a, b, dims):
    return lax.dot_general(a, b, (dims, ((), ())), preferred_element_type=F32)


NN = ((1,), (0,))
NT = ((1,), (1,))
TN = ((0,), (0,))


def params(**kw):
    return pltpu.CompilerParams(vmem_limit_bytes=VMEM_LIMIT, **kw)


def unit_norm(values):
    centered = values - jnp.mean(values, axis=-1, keepdims=True)
    inverse = lax.rsqrt(jnp.mean(centered * centered, axis=-1, keepdims=True) + EPS)
    return centered * inverse, inverse


def norm_back(grad, unit, inverse, gain):
    e = grad * gain
    inner = e - jnp.mean(e, axis=-1, keepdims=True) - unit * jnp.mean(e * unit, axis=-1, keepdims=True)
    return inner * inverse


def forward_kernel(
    x_ref, shift_in_ref, gain_ref, shift_ref, w_ref, b_ref, cos_ref, sin_ref,
    q_out, k_out, v_out, p_out, o_out, first_t_out, first_ref,
):
    group = pl.program_id(0)
    rows = q_out.shape[1]

    @pl.when(group == 0)
    def _():
        residual = x_ref[...].astype(F32) + shift_in_ref[...]
        unit, _ = unit_norm(residual)
        first = unit * gain_ref[0:1, :] + shift_ref[0:1, :]
        first_ref[...] = first.astype(BF)
        first_t_out[...] = first.T.astype(BF)

    half = HEAD_DIM // 2
    cos, sin = cos_ref[...], sin_ref[...]
    first = first_ref[...]
    query = dot(w_ref[0], first[:rows], NT) + b_ref[0]
    keys = dot(w_ref[1], first, NT) + b_ref[1]
    values = (dot(w_ref[2], first, NT) + b_ref[2]).astype(BF)
    v_out[...] = values

    def rotated(part, head, width):
        lo = part[head * HEAD_DIM : head * HEAD_DIM + half]
        hi = part[head * HEAD_DIM + half : (head + 1) * HEAD_DIM]
        c, s = cos[:, :width], sin[:, :width]
        return jnp.concatenate([lo * c - hi * s, hi * c + lo * s], axis=0)

    for head in range(HEADS_PER_STEP):
        at = slice(head * HEAD_DIM, (head + 1) * HEAD_DIM)
        q_t = (rotated(query, head, rows) * HEAD_DIM**-0.5).astype(BF)
        k_t = rotated(keys, head, first.shape[0])
        q_out[at, :] = q_t
        k_out[at, :] = k_t.astype(BF)
        scores = dot(k_t.T.astype(BF), q_t, NN)
        top = jnp.max(scores, axis=0, keepdims=True)
        weights = jnp.exp(scores - top)
        total = jnp.sum(weights, axis=0, keepdims=True)
        weights = (weights * (1.0 / total)).astype(BF)
        p_out[head] = weights
        o_out[at, :] = dot(values[at], weights, NN)


def attention_forward(x_all, start_row, gain, shift, w_t, b_cols, cos, sin):
    length, width = x_all.shape
    rows = length // lax.axis_size("seq")
    step = HEADS_PER_STEP * HEAD_DIM
    whole = lambda shape: pl.BlockSpec(shape, lambda g: (0,) * len(shape))
    return pl.pallas_call(
        forward_kernel,
        grid=(HEADS // HEADS_PER_STEP,),
        in_specs=[
            whole((length, width)),
            whole((1, width)),
            whole((2, width)),
            whole((2, width)),
            pl.BlockSpec((3, step, width), lambda g: (0, g, 0)),
            pl.BlockSpec((3, step, 1), lambda g: (0, g, 0)),
            whole(cos.shape),
            whole(sin.shape),
        ],
        out_specs=[
            pl.BlockSpec((step, rows), lambda g: (g, 0)),
            pl.BlockSpec((step, length), lambda g: (g, 0)),
            pl.BlockSpec((step, length), lambda g: (g, 0)),
            pl.BlockSpec((HEADS_PER_STEP, length, rows), lambda g: (g, 0, 0)),
            pl.BlockSpec((step, rows), lambda g: (g, 0)),
            whole((width, length)),
        ],
        out_shape=[
            jax.ShapeDtypeStruct((width, rows), BF),
            jax.ShapeDtypeStruct((width, length), BF),
            jax.ShapeDtypeStruct((width, length), BF),
            jax.ShapeDtypeStruct((HEADS, length, rows), BF),
            jax.ShapeDtypeStruct((width, rows), F32),
            jax.ShapeDtypeStruct((width, length), BF),
        ],
        scratch_shapes=[pltpu.VMEM((length, width), BF)],
        compiler_params=params(),
        name="attention_forward",
        cost_estimate=pl.CostEstimate(flops=6 * 10**9, bytes_accessed=20 * 10**6, transcendentals=3 * 10**6),
    )(x_all, start_row, gain, shift, w_t, b_cols, cos, sin)


def feed_kernel(
    o_ref, x_ref, start_ref, gain_ref, shift_ref, w_out_ref, b_out_ref, w_up_ref, b_up_ref,
    w_down_ref, b_down_ref, cot_ref,
    layer_ref, gmid_ref, do_ref, gdown_ref, gup_ref, small_ref, gbup_ref,
    middle_ref, unit_ref, inv_ref, second_ref, second_t_ref, acc_ref, gsec_ref,
):
    j = pl.program_id(0)
    last = pl.num_programs(0) - 1

    @pl.when(j == 0)
    def _():
        attended = o_ref[...].T.astype(BF)
        residual = x_ref[...].astype(F32) + start_ref[...]
        middle = residual + dot(attended, w_out_ref[...], NN) + b_out_ref[...]
        middle_ref[...] = middle
        unit, inverse = unit_norm(middle)
        unit_ref[...] = unit
        inv_ref[...] = inverse
        second = unit * gain_ref[1:2, :] + shift_ref[1:2, :]
        second_ref[...] = second.astype(BF)
        second_t_ref[...] = second.T.astype(BF)
        acc_ref[...] = jnp.zeros_like(acc_ref)
        gsec_ref[...] = jnp.zeros_like(gsec_ref)

    @pl.when(j < last)
    def _():
        cot = cot_ref[...]
        hidden = dot(second_ref[...], w_up_ref[...], NN) + b_up_ref[...]
        cdf = 0.5 + 0.5 * lax.erf(hidden * (0.5**0.5))
        active = (hidden * cdf).astype(BF)
        slope = cdf + hidden * (jnp.exp(-0.5 * hidden * hidden) * (1.0 / math.sqrt(2.0 * math.pi)))
        acc_ref[...] += dot(active, w_down_ref[...], NN)
        ghid = dot(cot, w_down_ref[...], NT) * slope
        ghid_low = ghid.astype(BF)
        gsec_ref[...] += dot(ghid_low, w_up_ref[...], NT)
        gdown_ref[...] = dot(active, cot, TN).astype(BF)
        gup_ref[0] = dot(second_t_ref[...], ghid_low, NN).astype(BF)
        gbup_ref[...] = jnp.sum(ghid_low.astype(F32), axis=0, keepdims=True)

    @pl.when(j == last)
    def _():
        cot = cot_ref[...].astype(F32)
        layer_ref[...] = (middle_ref[...] + acc_ref[...] + b_down_ref[...]).astype(BF)
        gsec, unit = gsec_ref[...], unit_ref[...]
        gmid = cot + norm_back(gsec, unit, inv_ref[...], gain_ref[1:2, :])
        gmid_ref[...] = gmid
        branch = gmid.astype(BF)
        gup_ref[0] = dot(o_ref[...].astype(BF), branch, NN).astype(BF)
        do_ref[...] = dot(w_out_ref[...], branch, NT).astype(BF)
        total = lambda v: jnp.sum(v, axis=0, keepdims=True)
        small_ref[0:1, :] = total(gsec * unit)
        small_ref[1:2, :] = total(gsec)
        small_ref[2:3, :] = total(branch.astype(F32))
        small_ref[3:4, :] = total(cot)


def feed_forward(o_t, x_own, start_row, gain, shift, w_out, b_out, w_up, b_up, w_down, b_down, cot):
    rows, width = x_own.shape
    hidden = w_up.shape[1]
    steps = hidden // width
    whole = lambda shape: pl.BlockSpec(shape, lambda j: (0,) * len(shape))
    held = lambda j: jnp.minimum(j, steps - 1)
    return pl.pallas_call(
        feed_kernel,
        grid=(steps + 1,),
        in_specs=[
            whole((width, rows)),
            whole((rows, width)),
            whole((1, width)),
            whole((2, width)),
            whole((2, width)),
            whole((width, width)),
            whole((1, width)),
            pl.BlockSpec((width, width), lambda j: (0, held(j))),
            pl.BlockSpec((1, width), lambda j: (0, held(j))),
            pl.BlockSpec((width, width), lambda j: (held(j), 0)),
            whole((1, width)),
            whole((rows, width)),
        ],
        out_specs=[
            whole((rows, width)),
            whole((rows, width)),
            whole((width, rows)),
            pl.BlockSpec((width, width), lambda j: (held(j), 0)),
            pl.BlockSpec((1, width, width), lambda j: (j, 0, 0)),
            whole((4, width)),
            pl.BlockSpec((1, width), lambda j: (0, held(j))),
        ],
        out_shape=[
            jax.ShapeDtypeStruct((rows, width), BF),
            jax.ShapeDtypeStruct((rows, width), F32),
            jax.ShapeDtypeStruct((width, rows), BF),
            jax.ShapeDtypeStruct((hidden, width), BF),
            jax.ShapeDtypeStruct((steps + 1, width, width), BF),
            jax.ShapeDtypeStruct((4, width), F32),
            jax.ShapeDtypeStruct((1, hidden), F32),
        ],
        scratch_shapes=[
            pltpu.VMEM((rows, width), F32),
            pltpu.VMEM((rows, width), F32),
            pltpu.VMEM((rows, 1), F32),
            pltpu.VMEM((rows, width), BF),
            pltpu.VMEM((width, rows), BF),
            pltpu.VMEM((rows, width), F32),
            pltpu.VMEM((rows, width), F32),
        ],
        compiler_params=params(),
        name="feed_forward",
        cost_estimate=pl.CostEstimate(flops=8 * 10**9, bytes_accessed=24 * 10**6, transcendentals=10**6),
    )(o_t, x_own, start_row, gain, shift, w_out, b_out, w_up, b_up, w_down, b_down, cot)


def backward_kernel(
    q_ref, k_ref, v_ref, p_ref, o_ref, do_ref, first_t_ref, w_ref, cos_ref, sin_ref,
    gqkv_ref, gb_ref, gx_own, gx_1, gx_2, gx_3,
    acc_ref, gq_ref, gk_ref, gv_ref,
):
    group = pl.program_id(0)
    rows = q_ref.shape[1]
    half = HEAD_DIM // 2
    cos, sin = cos_ref[...], sin_ref[...]

    def unrotated(part, width):
        lo, hi = part[:half], part[half:]
        c, s = cos[:, :width], sin[:, :width]
        return jnp.concatenate([lo * c + hi * s, hi * c - lo * s], axis=0)

    for head in range(HEADS_PER_STEP):
        at = slice(head * HEAD_DIM, (head + 1) * HEAD_DIM)
        do_t = do_ref[at, :]
        weights = p_ref[head]
        gweights = dot(v_ref[at, :].astype(F32).T.astype(BF), do_t, NN)
        inner = jnp.sum(do_t.astype(F32) * o_ref[at, :], axis=0, keepdims=True)
        gscores = (weights.astype(F32) * (gweights - inner)).astype(BF)
        gq = dot(k_ref[at, :], gscores, NN) * HEAD_DIM**-0.5
        gk = dot(q_ref[at, :], gscores, NT)
        gv_ref[at, :] = dot(do_t, weights, NT).astype(BF)
        gq_ref[at, :] = unrotated(gq, rows).astype(BF)
        gk_ref[at, :] = unrotated(gk, gk.shape[1]).astype(BF)

    gq, gk, gv = gq_ref[...], gk_ref[...], gv_ref[...]
    first_t = first_t_ref[...]
    gqkv_ref[0] = dot(first_t[:, :rows], gq, NT).astype(BF)
    gqkv_ref[1] = dot(first_t, gk, NT).astype(BF)
    gqkv_ref[2] = dot(first_t, gv, NT).astype(BF)
    ones = jnp.ones((8, gk.shape[1]), BF)
    gb_ref[0] = dot(ones[:, :rows], gq, NT)
    gb_ref[1] = dot(ones, gk, NT)
    gb_ref[2] = dot(ones, gv, NT)
    back = dot(w_ref[1], gk, NN) + dot(w_ref[2], gv, NN)
    own = dot(w_ref[0], gq, NN)

    @pl.when(group == 0)
    def _():
        acc_ref[...] = back

    @pl.when(group > 0)
    def _():
        acc_ref[...] += back

    acc_ref[:, :rows] += own

    @pl.when(group == pl.num_programs(0) - 1)
    def _():
        gx_own[...] = acc_ref[:, :rows]
        gx_1[...] = acc_ref[:, rows : 2 * rows].astype(BF)
        gx_2[...] = acc_ref[:, 2 * rows : 3 * rows].astype(BF)
        gx_3[...] = acc_ref[:, 3 * rows :].astype(BF)


def attention_backward(q_t, k_t, v_t, p_t, o_t, do_t, first_t, w_cols, cos, sin):
    width, rows = q_t.shape
    length = k_t.shape[1]
    step = HEADS_PER_STEP * HEAD_DIM
    whole = lambda shape: pl.BlockSpec(shape, lambda g: (0,) * len(shape))
    return pl.pallas_call(
        backward_kernel,
        grid=(HEADS // HEADS_PER_STEP,),
        in_specs=[
            pl.BlockSpec((step, rows), lambda g: (g, 0)),
            pl.BlockSpec((step, length), lambda g: (g, 0)),
            pl.BlockSpec((step, length), lambda g: (g, 0)),
            pl.BlockSpec((HEADS_PER_STEP, length, rows), lambda g: (g, 0, 0)),
            pl.BlockSpec((step, rows), lambda g: (g, 0)),
            pl.BlockSpec((step, rows), lambda g: (g, 0)),
            whole((width, length)),
            pl.BlockSpec((3, width, step), lambda g: (0, 0, g)),
            whole(cos.shape),
            whole(sin.shape),
        ],
        out_specs=[
            pl.BlockSpec((3, width, step), lambda g: (0, 0, g)),
            pl.BlockSpec((3, 8, step), lambda g: (0, 0, g)),
            whole((width, rows)),
            whole((width, rows)),
            whole((width, rows)),
            whole((width, rows)),
        ],
        out_shape=[
            jax.ShapeDtypeStruct((3, width, width), BF),
            jax.ShapeDtypeStruct((3, 8, width), F32),
            jax.ShapeDtypeStruct((width, rows), F32),
            jax.ShapeDtypeStruct((width, rows), BF),
            jax.ShapeDtypeStruct((width, rows), BF),
            jax.ShapeDtypeStruct((width, rows), BF),
        ],
        scratch_shapes=[
            pltpu.VMEM((width, length), F32),
            pltpu.VMEM((step, rows), BF),
            pltpu.VMEM((step, length), BF),
            pltpu.VMEM((step, length), BF),
        ],
        compiler_params=params(),
        name="attention_backward",
        cost_estimate=pl.CostEstimate(flops=12 * 10**9, bytes_accessed=30 * 10**6, transcendentals=0),
    )(q_t, k_t, v_t, p_t, o_t, do_t, first_t, w_cols, cos, sin)


def entry_kernel(g0_ref, g1_ref, g2_ref, g3_ref, x_ref, start_ref, gain_ref, gmid_ref, flag_ref, gtok_ref, small_ref):
    grad_t = g0_ref[...] + g1_ref[...].astype(F32) + g2_ref[...].astype(F32) + g3_ref[...].astype(F32)
    grad = grad_t.T
    residual = x_ref[...].astype(F32) + start_ref[...]
    unit, inverse = unit_norm(residual)
    gres = gmid_ref[...] + norm_back(grad, unit, inverse, gain_ref[0:1, :])
    gtok_ref[...] = gres.astype(BF)
    small_ref[0:1, :] = jnp.sum(grad * unit, axis=0, keepdims=True)
    small_ref[1:2, :] = jnp.sum(grad, axis=0, keepdims=True)
    small_ref[2:3, :] = jnp.sum(gres, axis=0, keepdims=True) * flag_ref[...]


def entry_backward(pieces, x_own, start_row, gain, gmid, flag_row):
    rows, width = x_own.shape
    return pl.pallas_call(
        entry_kernel,
        out_shape=[jax.ShapeDtypeStruct((rows, width), BF), jax.ShapeDtypeStruct((3, width), F32)],
        compiler_params=params(),
        name="entry_backward",
        cost_estimate=pl.CostEstimate(flops=10**7, bytes_accessed=4 * 10**6, transcendentals=0),
    )(*pieces, x_own, start_row, gain, gmid, flag_row)


BITS = {"c": ("dp", 1), "x": ("dp", 2), "y": ("dp", 4), "z": ("seq", 1), "w": ("seq", 2)}


def my_bit(name):
    axis, mask = BITS[name]
    return (lax.axis_index(axis) // mask) % 2


def other_bits():
    dp = lax.axis_size("dp")
    return [1 << k for k in range(3, dp.bit_length() - 1)]


def xor_pairs(size, mask):
    return [(i, i ^ mask) for i in range(size)]


def swap(value, names):
    dp, seq = lax.axis_size("dp"), lax.axis_size("seq")
    pairs = []
    for d in range(dp):
        axis, mask = BITS[names[d % 2]]
        for s in range(seq):
            to = (d ^ mask) * seq + s if axis == "dp" else d * seq + (s ^ mask)
            pairs.append((d * seq + s, to))
    return lax.ppermute(value, ("dp", "seq"), pairs)


def pick(array, index):
    return lax.dynamic_index_in_dim(array, index, 1, keepdims=False)


def scatter_sum(grads, orders):
    core = my_bit("c")
    parts = [grads.reshape(grads.shape[:1] + (2,) * 5 + grads.shape[2:])]
    for names in zip(*orders):
        bit = jnp.where(core == 0, my_bit(names[0]), my_bit(names[1]))
        send = sum(pick(p, 1 - bit).astype(F32) for p in parts).astype(BF)
        parts = [pick(p, bit) for p in parts] + [swap(send, names)]
    shard = sum(p.astype(F32) for p in parts)
    for mask in other_bits():
        shard = shard + lax.ppermute(shard.astype(BF), "dp", xor_pairs(lax.axis_size("dp"), mask)).astype(F32)
    return shard.astype(BF)


def gather_blocks(shard, orders):
    held = shard[:, None]
    for names in list(zip(*orders))[:0:-1]:
        held = jnp.concatenate([held, swap(held, names)], axis=1)
    return held, swap(held, ("c", "c"))


def place_of(orders):
    core = my_bit("c")
    low = []
    for order in orders:
        at = jnp.int32(0)
        for name in order[1:]:
            at = at * 2 + my_bit(name)
        low.append(at)
    own, other = jnp.where(core == 0, low[0], low[1]), jnp.where(core == 0, low[1], low[0])
    return jnp.stack([core, own, other]).astype(jnp.int32)


def all_sum(value):
    for axis in ("dp", "seq"):
        size = lax.axis_size(axis)
        for k in range(size.bit_length() - 1):
            value = value + lax.ppermute(value, axis, xor_pairs(size, 1 << k))
    return value


def spread_kernel(kind, at_ref, held_ref, other_ref, *outs):
    core = at_ref[0]
    held, other = held_ref[:, 0].astype(F32), other_ref[:, 0].astype(F32)
    for side in range(2):
        block = jnp.where(core == side, held, other)
        if kind == "heads":
            (out,) = outs
            two = 2 * HEAD_DIM
            for pair in range(HEADS // 2):
                q, k, v = (block[i, :, pair * two : (pair + 1) * two] for i in range(3))
                low = lambda a: a[:, :HEAD_DIM]
                high = lambda a: a[:, HEAD_DIM:]
                row = jnp.concatenate([low(q), low(k), low(v), high(q), high(k), high(v)], axis=1)
                out[side, 0, :, pair * 3 * two : (pair + 1) * 3 * two] = row
        else:
            width = block.shape[-1]
            main = outs[0]
            wide = main.shape[-1] // width
            for i in range(wide):
                main[side, 0, :, i * width : (i + 1) * width] = block[i]
            if len(outs) > 1:
                outs[1][side, 0] = block[wide]


def spread(kind, place, held, other, widths):
    n, half, rows, width = held.shape
    block = lambda who: pl.BlockSpec((n, 1, rows, width), lambda b, at: (0, b ^ at[who], 0, 0))
    outs = pl.pallas_call(
        lambda *refs: spread_kernel(kind, *refs),
        grid_spec=pltpu.PrefetchScalarGridSpec(
            num_scalar_prefetch=1,
            grid=(half,),
            in_specs=[block(1), block(2)],
            out_specs=[pl.BlockSpec((2, 1, rows, w), lambda b, at: (0, b, 0, 0)) for w in widths],
        ),
        out_shape=[jax.ShapeDtypeStruct((2, half, rows, w), F32) for w in widths],
        compiler_params=params(),
        name="spread_" + kind,
        cost_estimate=pl.CostEstimate(flops=0, bytes_accessed=12 * n * half * rows * width, transcendentals=0),
    )(place, held, other)
    return [o.reshape(2 * half * rows, w) for o, w in zip(outs, widths)]


ORDERS_DOWN = (("c", "x", "y", "z", "w"), ("c", "y", "x", "z", "w"))
ORDERS_UP = (("c", "x", "y", "z", "w"), ("c", "z", "x", "y", "w"))
ORDERS_HEADS = (("c", "y", "x", "z", "w"), ("c", "z", "y", "x", "w"))


def total_of(kind, grads, orders, widths):
    n, blocks = grads.shape[0], 32
    grads = grads.reshape(n, blocks, grads.shape[1] // blocks, grads.shape[2])
    held, other = gather_blocks(scatter_sum(grads, orders), orders)
    return spread(kind, place_of(orders), held, other, widths)


def per_device(
    tokens, codon_positions, start_flags, start_embed, norm_gain, norm_shift, w_qkv, b_qkv,
    w_out, b_out, w_up, b_up, w_down, b_down, cotangent,
):
    width = tokens.shape[-1]
    groups = lax.axis_size("seq")
    x_own, cot, positions = tokens[0], cotangent[0], codon_positions[0]
    flag = start_flags.astype(F32)
    start_row = flag[:, None] * start_embed[None, :]

    def everyone(value):
        return [value] + [lax.ppermute(value, "seq", xor_pairs(groups, k)) for k in range(1, groups)]

    positions = jnp.concatenate(everyone(positions))
    x_all = jnp.concatenate(everyone(x_own))
    half = HEAD_DIM // 2
    frequency = 10000.0 ** (-2.0 * jnp.arange(half, dtype=F32) / HEAD_DIM)
    angles = frequency[:, None] * positions.astype(F32)[None, :]
    cos, sin = jnp.cos(angles), jnp.sin(angles)
    by_head = w_qkv.reshape(width, HEADS, 3, HEAD_DIM)
    w_cols = by_head.transpose(2, 0, 1, 3).reshape(3, width, width)
    w_t = by_head.transpose(2, 1, 3, 0).reshape(3, width, width)
    b_cols = b_qkv.reshape(HEADS, 3, HEAD_DIM).transpose(1, 0, 2).reshape(3, width, 1)

    q_t, k_t, v_t, p_t, o_t, first_t = attention_forward(x_all, start_row, norm_gain, norm_shift, w_t, b_cols, cos, sin)
    layer_out, gmid, do_t, gdown, gup, small_feed, gbup = feed_forward(
        o_t, x_own, start_row, norm_gain, norm_shift, w_out, b_out[None], w_up, b_up[None], w_down, b_down[None], cot
    )
    (grad_down,) = total_of("down", gdown[None], ORDERS_DOWN, (width,))
    grad_up, grad_wout = total_of("up", gup, ORDERS_UP, (w_up.shape[1], width))
    gqkv, gbqkv, *pieces = attention_backward(q_t, k_t, v_t, p_t, o_t, do_t, first_t, w_cols, cos, sin)
    (grad_qkv,) = total_of("heads", gqkv, ORDERS_HEADS, (3 * width,))
    pieces = pieces[:1] + [lax.ppermute(piece, "seq", xor_pairs(groups, k + 1)) for k, piece in enumerate(pieces[1:])]
    grad_tokens, small_entry = entry_backward(pieces, x_own, start_row, norm_gain, gmid, flag[:, None])
    smalls = all_sum(jnp.concatenate([small_feed, gbup.reshape(-1, width), gbqkv[:, 0], small_entry]))
    gain_1, shift_1, grad_bout, grad_bdown = smalls[:4]
    grad_bup = smalls[4:-6].reshape(-1)
    grad_bqkv = smalls[-6:-3].reshape(3, HEADS, HEAD_DIM).transpose(1, 0, 2).reshape(-1)
    gain_0, shift_0, grad_start = smalls[-3:]
    return (
        layer_out[None],
        grad_tokens[None],
        grad_start,
        jnp.stack([gain_0, gain_1]),
        jnp.stack([shift_0, shift_1]),
        grad_qkv,
        grad_bqkv,
        grad_wout,
        grad_bout,
        grad_up,
        grad_bup,
        grad_down,
        grad_bdown,
    )


def solution(mesh):
    rows = P("dp", "seq", None)
    return jax.shard_map(
        per_device,
        mesh=mesh,
        in_specs=(rows, P("dp", "seq"), P("dp")) + (P(),) * 11 + (rows,),
        out_specs=(rows, rows) + (P(),) * 11,
        check_vma=False,
    )
```

```python
import math

import jax
import jax.numpy as jnp
from jax import lax
from jax.experimental import pallas as pl
from jax.experimental.pallas import tpu as pltpu
from jax.sharding import PartitionSpec as P

HEADS = 12
HEAD_DIM = 64
EPS = 1e-05
BF = jnp.bfloat16
F32 = jnp.float32
VMEM_LIMIT = 56 * 1024 * 1024
HEADS_PER_STEP = 4
LIGHT = pl.CostEstimate(flops=1, bytes_accessed=1, transcendentals=0)


def dot(a, b, dims):
    return lax.dot_general(a, b, (dims, ((), ())), preferred_element_type=F32)


NN = ((1,), (0,))
NT = ((1,), (1,))
TN = ((0,), (0,))


def params(**kw):
    return pltpu.CompilerParams(vmem_limit_bytes=VMEM_LIMIT, **kw)


def unit_norm(values):
    centered = values - jnp.mean(values, axis=-1, keepdims=True)
    inverse = lax.rsqrt(jnp.mean(centered * centered, axis=-1, keepdims=True) + EPS)
    return centered * inverse, inverse


def norm_back(grad, unit, inverse, gain):
    e = grad * gain
    inner = e - jnp.mean(e, axis=-1, keepdims=True) - unit * jnp.mean(e * unit, axis=-1, keepdims=True)
    return inner * inverse


def start_flag(x_ref, rows):
    return x_ref[0, rows : rows + 1, 2 * rows : 2 * rows + 1].astype(F32)


def table(ref):
    return jnp.concatenate([ref[i] for i in range(ref.shape[0])], axis=1)


def forward_kernel(
    x_ref, shift_in_ref, gain_ref, shift_ref, w_ref, b_ref, cos_ref, sin_ref,
    q_out, k_out, v_out, p_out, o_out, first_t_out, first_ref,
):
    group = pl.program_id(0)
    rows = q_out.shape[1]

    @pl.when(group == 0)
    def _():
        x = jnp.concatenate([x_ref[i, :rows] for i in range(x_ref.shape[0])], axis=0)
        residual = x.astype(F32) + start_flag(x_ref, rows) * shift_in_ref[...]
        unit, _ = unit_norm(residual)
        first = unit * gain_ref[0:1, :] + shift_ref[0:1, :]
        first_ref[...] = first.astype(BF)
        first_t_out[...] = first.astype(BF).T

    half = HEAD_DIM // 2
    cos, sin = table(cos_ref), table(sin_ref)
    first = first_ref[...]
    query = dot(w_ref[0], first[:rows], NT) + b_ref[0]
    keys = dot(w_ref[1], first, NT) + b_ref[1]
    values = (dot(w_ref[2], first, NT) + b_ref[2]).astype(BF)
    v_out[...] = values

    def rotated(part, head, width):
        lo = part[head * HEAD_DIM : head * HEAD_DIM + half]
        hi = part[head * HEAD_DIM + half : (head + 1) * HEAD_DIM]
        c, s = cos[:, :width], sin[:, :width]
        return jnp.concatenate([lo * c - hi * s, hi * c + lo * s], axis=0)

    for head in range(HEADS_PER_STEP):
        at = slice(head * HEAD_DIM, (head + 1) * HEAD_DIM)
        q_t = (rotated(query, head, rows) * HEAD_DIM**-0.5).astype(BF)
        k_t = rotated(keys, head, first.shape[0])
        q_out[at, :] = q_t
        k_out[at, :] = k_t.astype(BF)
        scores = dot(k_t.T.astype(BF), q_t, NN)
        top = jnp.max(scores, axis=0, keepdims=True)
        weights = jnp.exp(scores - top)
        total = jnp.sum(weights, axis=0, keepdims=True)
        weights = (weights * (1.0 / total)).astype(BF)
        p_out[head] = weights
        o_out[at, :] = dot(values[at], weights, NN)


def attention_forward(x_all, start_row, gain, shift, w_t, b_cols, cos, sin):
    rows, width = cos.shape[2], x_all.shape[2]
    length = cos.shape[0] * rows
    step = HEADS_PER_STEP * HEAD_DIM
    whole = lambda shape: pl.BlockSpec(shape, lambda g: (0,) * len(shape))
    return pl.pallas_call(
        forward_kernel,
        grid=(HEADS // HEADS_PER_STEP,),
        in_specs=[
            whole(x_all.shape),
            whole((1, width)),
            whole((2, width)),
            whole((2, width)),
            pl.BlockSpec((3, step, width), lambda g: (0, g, 0)),
            pl.BlockSpec((3, step, 1), lambda g: (0, g, 0)),
            whole(cos.shape),
            whole(sin.shape),
        ],
        out_specs=[
            pl.BlockSpec((step, rows), lambda g: (g, 0)),
            pl.BlockSpec((step, length), lambda g: (g, 0)),
            pl.BlockSpec((step, length), lambda g: (g, 0)),
            pl.BlockSpec((HEADS_PER_STEP, length, rows), lambda g: (g, 0, 0)),
            pl.BlockSpec((step, rows), lambda g: (g, 0)),
            whole((width, length)),
        ],
        out_shape=[
            jax.ShapeDtypeStruct((width, rows), BF),
            jax.ShapeDtypeStruct((width, length), BF),
            jax.ShapeDtypeStruct((width, length), BF),
            jax.ShapeDtypeStruct((HEADS, length, rows), BF),
            jax.ShapeDtypeStruct((width, rows), F32),
            jax.ShapeDtypeStruct((width, length), BF),
        ],
        scratch_shapes=[pltpu.VMEM((length, width), BF)],
        compiler_params=params(),
        name="attention_forward",
        cost_estimate=LIGHT,
    )(x_all, start_row, gain, shift, w_t, b_cols, cos, sin)


def whole(shape):
    return pl.BlockSpec(shape, lambda *_: (0,) * len(shape))


def feed_chunk(second, second_t, cot, w_up, b_up, w_down):
    hidden = dot(second, w_up, NN) + b_up
    cdf = 0.5 + 0.5 * lax.erf(hidden * (0.5**0.5))
    active = (hidden * cdf).astype(BF)
    slope = cdf + hidden * (jnp.exp(-0.5 * hidden * hidden) * (1.0 / math.sqrt(2.0 * math.pi)))
    out = dot(active, w_down, NN)
    ghid = (dot(cot, w_down, NT) * slope).astype(BF)
    gsec = dot(ghid, w_up, NT)
    gdown = dot(active, cot, TN).astype(BF)
    gup = dot(second_t, ghid, NN).astype(BF)
    return out, gsec, gdown, gup, jnp.sum(ghid.astype(F32), axis=0, keepdims=True)


def store_blocks(out_ref, value, at_ref, base):
    rows = out_ref.shape[2]
    for block in range(8):
        place = block ^ (at_ref[base + 1] * 4 + at_ref[base + 2] * 2 + at_ref[base + 3])
        out_ref[0, place] = value[block * rows : (block + 1) * rows]


def feed_first_kernel(
    at_ref, o_ref, x_ref, start_ref, gain_ref, shift_ref, w_out_ref, b_out_ref, w_up_ref, b_up_ref, w_down_ref, cot_ref,
    middle_ref, second_ref, second_t_ref, acc_ref, gsec_ref, gdown_ref, gup_ref, gbup_ref,
):
    @pl.when(pl.program_id(0) == 0)
    def _():
        attended = o_ref[...].T.astype(BF)
        rows = o_ref.shape[1]
        residual = x_ref[0, :rows].astype(F32) + start_flag(x_ref, rows) * start_ref[...]
        middle = residual + dot(attended, w_out_ref[...], NN) + b_out_ref[...]
        middle_ref[...] = middle
        unit, _ = unit_norm(middle)
        second = unit * gain_ref[1:2, :] + shift_ref[1:2, :]
        second_ref[...] = second.astype(BF)
        second_t_ref[...] = second.T.astype(BF)
        acc_ref[...] = jnp.zeros_like(acc_ref)
        gsec_ref[...] = jnp.zeros_like(gsec_ref)

    out, gsec, gdown, gup, gbup_ref[0] = feed_chunk(
        second_ref[...], second_t_ref[...], cot_ref[...], w_up_ref[...], b_up_ref[...], w_down_ref[...]
    )
    store_blocks(gdown_ref, gdown, at_ref, 5)
    store_blocks(gup_ref, gup, at_ref, 5)
    acc_ref[...] += out
    gsec_ref[...] += gsec


def feed_second_kernel(
    at_ref, middle_ref, second_ref, second_t_ref, acc_in_ref, gsec_in_ref, gain_ref, w_out_ref, w_up_ref, b_up_ref,
    w_down_ref, b_down_ref, cot_ref,
    layer_ref, gmid_ref, branch_ref, do_ref, gdown_ref, gup_ref, gbup_ref, small_ref,
    acc_ref, gsec_ref,
):
    s = pl.program_id(0)

    @pl.when(s == 0)
    def _():
        acc_ref[...] = acc_in_ref[...]
        gsec_ref[...] = gsec_in_ref[...]

    out, gsec, gdown, gup, gbup_ref[0] = feed_chunk(
        second_ref[...], second_t_ref[...], cot_ref[...], w_up_ref[...], b_up_ref[...], w_down_ref[...]
    )
    store_blocks(gdown_ref, gdown, at_ref, 1)
    store_blocks(gup_ref, gup, at_ref, 1)
    acc_ref[...] += out
    gsec_ref[...] += gsec

    @pl.when(s == pl.num_programs(0) - 1)
    def _():
        cot = cot_ref[...].astype(F32)
        middle = middle_ref[...]
        unit, inverse = unit_norm(middle)
        layer_ref[...] = (middle + acc_ref[...] + b_down_ref[...]).astype(BF)
        gsec = gsec_ref[...]
        gmid = cot + norm_back(gsec, unit, inverse, gain_ref[1:2, :])
        gmid_ref[...] = gmid
        branch = gmid.astype(BF)
        branch_ref[...] = branch
        do_ref[...] = dot(w_out_ref[...], branch, NT).astype(BF)
        total = lambda v: jnp.sum(v, axis=0, keepdims=True)
        small_ref[0:1, :] = total(gsec * unit)
        small_ref[1:2, :] = total(gsec)
        small_ref[2:3, :] = total(branch.astype(F32))
        small_ref[3:4, :] = total(cot)


def feed_forward(at, o_t, x_all, start_row, gain, shift, w_out, b_out, w_up, b_up, w_down, b_down, cot):
    rows, width = cot.shape
    steps = w_up.shape[1] // width // 2
    shape = lambda *dims, kind=F32: jax.ShapeDtypeStruct(dims, kind)

    def chunk_specs(theirs):
        chunk = lambda s, at: (steps * jnp.where(theirs, 1 - at[0], at[0]) + s)
        return [
            pl.BlockSpec((width, width), lambda s, at: (0, chunk(s, at))),
            pl.BlockSpec((1, width), lambda s, at: (0, chunk(s, at))),
            pl.BlockSpec((width, width), lambda s, at: (chunk(s, at), 0)),
        ]

    def grad_specs(base):
        block = pl.BlockSpec((1, 8, width // 8, width), lambda s, at: (s ^ at[base], 0, 0, 0))
        return [
            block,
            block,
            pl.BlockSpec((1, 1, width), lambda s, at: (s, 0, 0)),
        ]

    grad_shapes = [shape(steps, 8, width // 8, width, kind=BF)] * 2 + [shape(steps, 1, width)]
    full, turned = whole((rows, width)), whole((width, rows))
    cost = LIGHT
    middle, second, second_t, acc, gsec, *theirs = pl.pallas_call(
        feed_first_kernel,
        grid_spec=pltpu.PrefetchScalarGridSpec(
            num_scalar_prefetch=1,
            grid=(steps,),
            in_specs=[
                turned, whole((1,) + x_all.shape[1:]), whole((1, width)), whole((2, width)), whole((2, width)), whole((width, width)),
                whole((1, width)), *chunk_specs(True), full,
            ],
            out_specs=[full, full, turned, full, full, *grad_specs(5)],
        ),
        out_shape=[
            shape(rows, width), shape(rows, width, kind=BF), shape(width, rows, kind=BF), shape(rows, width),
            shape(rows, width), *grad_shapes,
        ],
        compiler_params=params(),
        name="feed_first",
        cost_estimate=cost,
    )(at, o_t, x_all, start_row, gain, shift, w_out, b_out, w_up, b_up, w_down, cot)
    layer, gmid, branch, do_t, *mine, small = pl.pallas_call(
        feed_second_kernel,
        grid_spec=pltpu.PrefetchScalarGridSpec(
            num_scalar_prefetch=1,
            grid=(steps,),
            in_specs=[
                full, full, turned, full, full, whole((2, width)), whole((width, width)), *chunk_specs(False),
                whole((1, width)), full,
            ],
            out_specs=[full, full, full, turned, *grad_specs(1), whole((4, width))],
            scratch_shapes=[pltpu.VMEM((rows, width), F32), pltpu.VMEM((rows, width), F32)],
        ),
        out_shape=[
            shape(rows, width, kind=BF), shape(rows, width), shape(rows, width, kind=BF), shape(width, rows, kind=BF),
            *grad_shapes, shape(4, width),
        ],
        compiler_params=params(),
        name="feed_second",
        cost_estimate=cost,
    )(at, middle, second, second_t, acc, gsec, gain, w_out, w_up, b_up, w_down, b_down, cot)
    return layer, gmid, branch, do_t, theirs, mine, small


def backward_kernel(
    q_ref, k_ref, v_ref, p_ref, o_ref, do_ref, cos_ref, sin_ref, gq_ref, gk_ref, gv_ref, gb_ref,
):
    rows = q_ref.shape[1]
    half = HEAD_DIM // 2
    cos, sin = table(cos_ref), table(sin_ref)

    def unrotated(part, width):
        lo, hi = part[:half], part[half:]
        c, s = cos[:, :width], sin[:, :width]
        return jnp.concatenate([lo * c + hi * s, hi * c - lo * s], axis=0)

    gqs, gks, gvs = [], [], []
    for head in range(HEADS_PER_STEP):
        at = slice(head * HEAD_DIM, (head + 1) * HEAD_DIM)
        do_t = do_ref[at, :]
        weights = p_ref[head]
        gweights = dot(v_ref[at, :].T, do_t, NN)
        inner = jnp.sum(do_t.astype(F32) * o_ref[at, :], axis=0, keepdims=True)
        gscores = (weights.astype(F32) * (gweights - inner)).astype(BF)
        gq = dot(k_ref[at, :], gscores, NN) * HEAD_DIM**-0.5
        gk = dot(gscores, q_ref[at, :].T, NN)
        gvs.append(dot(weights, do_t.T, NN).astype(BF))
        gqs.append(unrotated(gq, rows).astype(BF))
        gks.append(unrotated(gk.T, gk.shape[0]).astype(BF))
    gq_ref[...] = jnp.concatenate(gqs, axis=0).T
    gk_ref[...] = jnp.concatenate(gks, axis=0).T
    gv_ref[...] = jnp.concatenate(gvs, axis=1)
    ones = jnp.ones((8, gk_ref.shape[0]), BF)
    gb_ref[0] = dot(ones[:, :rows], gq_ref[...], NN)
    gb_ref[1] = dot(ones, gk_ref[...], NN)
    gb_ref[2] = dot(ones, gv_ref[...], NN)


def attention_backward(q_t, k_t, v_t, p_t, o_t, do_t, cos, sin):
    width, rows = q_t.shape
    length = k_t.shape[1]
    step = HEADS_PER_STEP * HEAD_DIM
    narrow, wide = pl.BlockSpec((step, rows), lambda g: (g, 0)), pl.BlockSpec((step, length), lambda g: (g, 0))
    return pl.pallas_call(
        backward_kernel,
        grid=(HEADS // HEADS_PER_STEP,),
        in_specs=[
            narrow, wide, wide, pl.BlockSpec((HEADS_PER_STEP, length, rows), lambda g: (g, 0, 0)), narrow, narrow,
            whole(cos.shape), whole(sin.shape),
        ],
        out_specs=[pl.BlockSpec((n, step), lambda g: (0, g)) for n in (rows, length, length)]
        + [pl.BlockSpec((3, 8, step), lambda g: (0, 0, g))],
        out_shape=[
            jax.ShapeDtypeStruct((rows, width), BF),
            jax.ShapeDtypeStruct((length, width), BF),
            jax.ShapeDtypeStruct((length, width), BF),
            jax.ShapeDtypeStruct((3, 8, width), F32),
        ],
        compiler_params=params(),
        name="attention_backward",
        cost_estimate=LIGHT,
    )(q_t, k_t, v_t, p_t, o_t, do_t, cos, sin)


def head_grads(store, side, base, at_ref, gq_ref, gk_ref, gv_ref, first_t_ref, o_ref, branch_ref):
    rows = gq_ref.shape[0]
    part = first_t_ref.shape[0] // 2
    size = part // 4
    group = at_ref[base] * 2 + at_ref[base + 1]
    mat = at_ref[base + 2] * 2 + at_ref[base + 3]
    at = [pl.ds(pl.multiple_of(side * part + (place ^ group) * size, 32), size) for place in range(4)]
    first_t = jnp.concatenate([first_t_ref[where, :] for where in at], axis=0)
    attended = jnp.concatenate([o_ref[where, :] for where in at], axis=0).astype(BF)
    grads = (
        dot(first_t[:, :rows], gq_ref[...], NN),
        dot(first_t, gk_ref[...], NN),
        dot(first_t, gv_ref[...], NN),
        dot(attended, branch_ref[...], NN),
    )
    for i, grad in enumerate(grads):
        for place in range(4):
            store(place, i ^ mat, grad[place * size : (place + 1) * size].astype(BF))


def heads_first_kernel(at_ref, gq_ref, gk_ref, gv_ref, first_t_ref, o_ref, branch_ref, *outs):
    def store(place, mat, value):
        outs[place][mat] = value

    head_grads(store, 1 - at_ref[0], 5, at_ref, gq_ref, gk_ref, gv_ref, first_t_ref, o_ref, branch_ref)


def heads_second_kernel(
    at_ref, gq_ref, gk_ref, gv_ref, first_t_ref, o_ref, branch_ref, w_ref,
    mine_ref, gx_own, gx_near, gx_core, acc_ref,
):
    group = pl.program_id(0)
    rows = gq_ref.shape[0]
    back = dot(gk_ref[...], w_ref[1], NN) + dot(gv_ref[...], w_ref[2], NN)
    own = dot(gq_ref[...], w_ref[0], NN)

    @pl.when(group == 0)
    def _():
        acc_ref[...] = back

    @pl.when(group > 0)
    def _():
        acc_ref[...] += back

    acc_ref[:rows] += own

    def store(place, mat, value):
        mine_ref[place, mat] = value

    head_grads(store, at_ref[0], 1, at_ref, gq_ref, gk_ref, gv_ref, first_t_ref, o_ref, branch_ref)

    @pl.when(group == pl.num_programs(0) - 1)
    def _():
        gx_own[...] = acc_ref[:rows]
        gx_near[...] = acc_ref[rows : 2 * rows]
        gx_core[...] = acc_ref[2 * rows :].astype(BF)


def heads_specs(rows, width, length):
    step = HEADS_PER_STEP * HEAD_DIM
    column = lambda n: pl.BlockSpec((n, step), lambda g, at: (0, g))
    ins = [column(rows), column(length), column(length), whole((width, length)), whole((width, rows)), column(rows)]
    grad = pl.BlockSpec((4, 4, width // 8, step), lambda g, at: (0, 0, 0, g))
    return ins, grad, jax.ShapeDtypeStruct((4, 4, width // 8, width), BF)


def heads_first(at, gq, gk, gv, first_t, o_t, branch):
    rows, width = gq.shape
    ins, _, _ = heads_specs(rows, width, gk.shape[0])
    piece = pl.BlockSpec((4, width // 8, HEADS_PER_STEP * HEAD_DIM), lambda g, at: (0, 0, g))
    return pl.pallas_call(
        heads_first_kernel,
        grid_spec=pltpu.PrefetchScalarGridSpec(
            num_scalar_prefetch=1, grid=(HEADS // HEADS_PER_STEP,), in_specs=ins, out_specs=[piece] * 4
        ),
        out_shape=[jax.ShapeDtypeStruct((4, width // 8, width), BF)] * 4,
        compiler_params=params(),
        name="heads_first",
        cost_estimate=LIGHT,
    )(at, gq, gk, gv, first_t, o_t, branch)


def heads_second(at, gq, gk, gv, first_t, o_t, branch, w_t):
    rows, width = gq.shape
    ins, grad, shape = heads_specs(rows, width, gk.shape[0])
    step = HEADS_PER_STEP * HEAD_DIM
    piece = lambda kind, n: jax.ShapeDtypeStruct((n * rows, width), kind)
    return pl.pallas_call(
        heads_second_kernel,
        grid_spec=pltpu.PrefetchScalarGridSpec(
            num_scalar_prefetch=1,
            grid=(HEADS // HEADS_PER_STEP,),
            in_specs=ins + [pl.BlockSpec((3, step, width), lambda g, at: (0, g, 0))],
            out_specs=[grad, whole((rows, width)), whole((rows, width)), whole((2 * rows, width))],
            scratch_shapes=[pltpu.VMEM((gk.shape[0], width), F32)],
        ),
        out_shape=[shape, piece(F32, 1), piece(F32, 1), piece(BF, 2)],
        compiler_params=params(),
        name="heads_second",
        cost_estimate=LIGHT,
    )(at, gq, gk, gv, first_t, o_t, branch, w_t)


def entry_kernel(own_ref, core_ref, near_ref, x_ref, start_ref, gain_ref, gmid_ref, gtok_ref, small_ref):
    rows = own_ref.shape[0]
    grad = own_ref[...] + core_ref[:rows].astype(F32) + near_ref[...].astype(F32)
    flag = start_flag(x_ref, rows)
    unit, inverse = unit_norm(x_ref[0, :rows].astype(F32) + flag * start_ref[...])
    gres = gmid_ref[...] + norm_back(grad, unit, inverse, gain_ref[0:1, :])
    gtok_ref[...] = gres.astype(BF)
    small_ref[0:1, :] = jnp.sum(grad * unit, axis=0, keepdims=True)
    small_ref[1:2, :] = jnp.sum(grad, axis=0, keepdims=True)
    small_ref[2:3, :] = jnp.sum(gres, axis=0, keepdims=True) * flag


def entry_backward(pieces, x_all, start_row, gain, gmid):
    rows, width = gmid.shape
    ins = [*pieces, x_all, start_row, gain, gmid]
    specs = [whole(a.shape) for a in ins]
    specs[len(pieces)] = whole((1,) + x_all.shape[1:])
    return pl.pallas_call(
        entry_kernel,
        grid=(1,),
        in_specs=specs,
        out_specs=[whole((rows, width)), whole((3, width))],
        out_shape=[jax.ShapeDtypeStruct((rows, width), BF), jax.ShapeDtypeStruct((3, width), F32)],
        compiler_params=params(),
        name="entry_backward",
        cost_estimate=LIGHT,
    )(*ins)


BITS = {"c": ("dp", 1), "x": ("dp", 2), "y": ("dp", 4), "z": ("seq", 1), "w": ("seq", 2)}
ORDER = ("xywz", "yxwz")
LEVELS = {"a": "xy", "b": "yx", "w": "ww", "z": "zz"}


def my_bit(name):
    axis, mask = BITS[name]
    return (lax.axis_index(axis) // mask) % 2


def xor_pairs(size, mask):
    return [(i, i ^ mask) for i in range(size)]


def swap(value, names):
    dp, seq = lax.axis_size("dp"), lax.axis_size("seq")
    pairs = []
    for d in range(dp):
        axis, mask = BITS[names[d % 2]]
        for s in range(seq):
            to = (d ^ mask) * seq + s if axis == "dp" else d * seq + (s ^ mask)
            pairs.append((d * seq + s, to))
    return lax.ppermute(value, ("dp", "seq"), pairs)


def swap_seq(value, mask):
    return lax.ppermute(value, "seq", xor_pairs(lax.axis_size("seq"), mask))


def numbers():
    core = my_bit("c")
    first, second = ([my_bit(name) for name in order] for order in ORDER)
    pick = lambda a, b: jnp.where(core == 0, a, b)
    bits = [pick(a, b) for a, b in zip(first, second)] + [pick(b, a) for a, b in zip(first, second)]
    return jnp.stack([core] + bits).astype(jnp.int32)


class Chain:
    def __init__(self, last):
        self.last = last

    def then(self, step, *args):
        args, _ = lax.optimization_barrier((args, self.last))
        self.last = step(*args)
        return self.last


def add_up(parts):
    return sum(p.astype(F32) for p in parts).astype(BF)


class Part:
    def __init__(self, value, bits):
        self.value, self.bits = value, bits

    def take(self, value, sides):
        if isinstance(value, tuple):
            size = 2 if self.bits[1] in sides else 1
            first = 2 * sides[self.bits[0]] + sides.get(self.bits[1], 0)
            picked = value[first : first + 1] if size == 2 else value[first : first + 2]
            rest = {bit: side for bit, side in sides.items() if bit not in self.bits[:2]}
            inner = [Part(v, self.bits[2:]).take(v, rest) for v in picked]
            return inner[0] if size == 2 else jnp.stack(inner)
        index = tuple(sides[bit] if bit in sides else slice(None) for bit in self.bits)
        return value.reshape((2,) * len(self.bits) + value.shape[-2:])[index]


class Chunk:
    def __init__(self, theirs, received, mine):
        rows, width = mine.shape[-2:]
        blocks = lambda a: a if isinstance(a, tuple) else a.reshape((16, rows, width))
        self.parts = [Part(blocks(mine), "abwz"), Part(blocks(received), "abwz")]
        self.done = {}

    def step(self, chain, choices):
        parts, done = list(self.parts), dict(self.done)

        def sums(*values):
            out = []
            for choice in choices:
                sides = {**done, **choice}
                taken = [
                    part.take(v, {bit: side for bit, side in sides.items() if bit in part.bits})
                    for part, v in zip(parts, values)
                ]
                out.append(add_up(taken))
            return tuple(out)

        return chain.then(sums, *(part.value for part in parts))

    def halve(self, chain, bit):
        (send,) = self.step(chain, [{bit: 1}])
        self.done[bit] = 0
        left = "".join(b for b in "abwz" if b not in self.done)
        self.parts.append(Part(swap(send, LEVELS[bit]), left))

    def quarter(self, chain):
        seq = lax.axis_size("seq")
        sends = self.step(chain, [{"w": k // 2, "z": k % 2} for k in range(1, seq)])
        self.done.update(w=0, z=0)
        left = "".join(b for b in "abwz" if b not in self.done)
        self.parts += [Part(swap_seq(send, k + 1), left) for k, send in enumerate(sends)]

    def finish(self, chain):
        (held,) = self.step(chain, [{}])
        held = held[None]
        dp = lax.axis_size("dp")
        for k in range(3, dp.bit_length() - 1):
            other = lax.ppermute(held, "dp", xor_pairs(dp, 1 << k))
            held = chain.then(lambda a, b: add_up([a, b]), held, other)
        return held


class Gather:
    def __init__(self, chain, shards):
        self.held = shards[0][None] if len(shards) == 1 else chain.then(lambda *a: jnp.stack(a), *shards)
        self.received = [swap_seq(self.held, k) for k in range(1, lax.axis_size("seq"))]
        self.levels = ["a", "b"]

    def double(self, chain):
        self.held = chain.then(lambda *parts: jnp.concatenate(parts, axis=1), self.held, *self.received)
        self.received = [swap(self.held, LEVELS[self.levels.pop()])]
        if not self.levels:
            self.others = [swap(self.held, "cc")]

    def cross(self, chain):
        received, _ = lax.optimization_barrier((self.received[0], chain.last))
        chain.last = received
        self.others.append(swap(received, "cc"))

    def spread(self, chain, kind, i):
        ins = [self.held, self.received[0], *self.others]
        at = numbers()
        return chain.then(lambda *ins: spread(kind, i, at, list(ins)), *ins)


def sum_small(chain, value, axis, masks):
    size = lax.axis_size(axis)
    parts = [lax.ppermute(value, axis, xor_pairs(size, mask)) for mask in masks]
    return chain.then(lambda *parts: sum(parts), value, *parts)


def spread_kernel(kind, at_ref, *refs):
    ins, outs = refs[:4], refs[4:]
    core = at_ref[0]
    for half in range(2):
        side = core if half == 0 else 1 - core
        b3, b2, b1, b0 = (at_ref[1 + 4 * half + i] for i in range(4))
        for top in range(2):
            src = ins[2 * half + top]
            hi = b3 if top == 0 else 1 - b3
            if kind == "heads":
                for i in range(4):
                    outs[2][side, hi, i ^ (b1 * 2 + b0)] = src[0, i].astype(F32)
                continue
            for i in range(2):
                if kind == "down":
                    outs[0][side, hi, 0, i ^ b0] = src[0, i].astype(F32)
                else:
                    width = src.shape[-1]
                    col = pl.multiple_of((side * 2 + hi) * width, width)
                    outs[0][0, i ^ b0, :, pl.ds(col, width)] = src[0, i].astype(F32)
    if kind == "heads":
        w_qkv, w_out, natural = outs
        for side in range(2):
            for hi in range(2):
                w_out[side, hi, 0] = natural[side, hi, 3]
                q, k, v = (natural[side, hi, i] for i in range(3))
                cuts = [slice(h * HEAD_DIM, (h + 1) * HEAD_DIM) for h in range(q.shape[1] // HEAD_DIM)]
                w_qkv[side, hi, 0] = jnp.concatenate([m[:, cut] for cut in cuts for m in (q, k, v)], axis=1)


def spread(kind, which, at, ins):
    n, _, rows, width = ins[0].shape
    scratch, grid = [], (4,)
    if kind == "heads":
        ins = [a.reshape(n, 2, 4, rows, width) for a in ins]
        grid = (2, 2)
        part = width // 2
        spec = lambda base: pl.BlockSpec(
            (None, 1, 4, rows, part), lambda p, c, at: (which, p ^ at[base + 1], 0, 0, c)
        )
        outs = [(2, 2, 2, rows, 3 * width), (2, 2, 2, rows, width)]
        blocks = [pl.BlockSpec((2, 2, 1, rows, o[4] // 2), lambda p, c, at: (0, 0, p, 0, c)) for o in outs]
        scratch = [pltpu.VMEM((2, 2, 4, rows, part), F32)]
    else:
        ins = [a.reshape(n, 4, 2, rows, width) for a in ins]
        low = lambda base, p, at: p ^ (at[base + 1] * 2 + at[base + 2])
        spec = lambda base: pl.BlockSpec((None, 1, 2, rows, width), lambda p, at: (which, low(base, p, at), 0, 0, 0))
        if kind == "down":
            outs = [(2, 2, 4, 2, rows, width)]
            blocks = [pl.BlockSpec((2, 2, 1, 2, rows, width), lambda p, at: (0, 0, p, 0, 0, 0))]
        else:
            outs = [(4, 2, rows, 4 * width)]
            blocks = [pl.BlockSpec((1, 2, rows, 4 * width), lambda p, at: (p, 0, 0, 0))]
    made = pl.pallas_call(
        lambda *refs: spread_kernel(kind, *refs),
        grid_spec=pltpu.PrefetchScalarGridSpec(
            num_scalar_prefetch=1,
            grid=grid,
            in_specs=[spec(1), spec(1), spec(5), spec(5)],
            out_specs=blocks,
            scratch_shapes=scratch,
        ),
        out_shape=[jax.ShapeDtypeStruct(o, F32) for o in outs],
        compiler_params=params(),
        name="spread_" + kind,
        cost_estimate=LIGHT,
    )(at, *ins)
    return [m.reshape(-1, m.shape[-1]) for m in made]


class Homes:
    def __init__(self):
        self.dp, self.seq = lax.axis_size("dp"), lax.axis_size("seq")
        self.native = (lax.axis_index("seq") // 2) % 2 == my_bit("c")

    def pairs(self, native_step, foreign_step):
        out = []
        for d in range(self.dp):
            for z in range(self.seq):
                step = native_step if z // 2 % 2 == d % 2 else foreign_step
                if step is not None:
                    swap_core, mask = step
                    out.append((d * self.seq + z, (d ^ swap_core) * self.seq + (z ^ mask)))
        return out

    def move(self, value, native_step, foreign_step):
        return lax.ppermute(value, ("dp", "seq"), self.pairs(native_step, foreign_step))

    def settle(self, value):
        return jnp.where(self.native, value, self.move(value, None, (1, 2)))

    def gather(self, tokens, positions, flag, meanwhile):
        rows, width = tokens.shape
        digits = jnp.concatenate([positions // 64, positions % 64, flag]).astype(BF)
        extra = jnp.pad(digits, (0, width - digits.shape[0]))
        value = jnp.concatenate([tokens, jnp.broadcast_to(extra, (8, width))])
        far = self.move(value, None, (1, 3))
        near = self.move(value, (0, 1), (1, 2))
        (near, far), meanwhile = lax.optimization_barrier(((near, far), meanwhile))
        two = jnp.stack([jnp.where(self.native, value, near), jnp.where(self.native, near, far)])
        four = jnp.concatenate([two, swap(two, "cc")])
        return four, meanwhile


def per_device(
    tokens, codon_positions, start_flags, start_embed, norm_gain, norm_shift, w_qkv, b_qkv,
    w_out, b_out, w_up, b_up, w_down, b_down, cotangent,
):
    width = tokens.shape[-1]
    core = my_bit("c").astype(jnp.int32)
    at = numbers()
    homes = Homes()
    by_head = w_qkv.reshape(width, HEADS, 3, HEAD_DIM)
    w_t = by_head.transpose(2, 1, 3, 0).reshape(3, width, width)
    b_cols = b_qkv.reshape(HEADS, 3, HEAD_DIM).transpose(1, 0, 2).reshape(3, width, 1)
    rows = tokens.shape[1]
    x_all, (w_t, b_cols) = homes.gather(tokens[0], codon_positions[0], start_flags, (w_t, b_cols))
    cot_moved = homes.move(cotangent[0], None, (1, 2))
    half = HEAD_DIM // 2
    frequency = 10000.0 ** (-2.0 * jnp.arange(half, dtype=F32) / HEAD_DIM)
    digits = x_all[:, rows, : 2 * rows].astype(F32)
    angles = frequency[None, :, None] * (digits[:, :rows] * 64 + digits[:, rows:])[:, None, :]
    cos, sin = jnp.cos(angles), jnp.sin(angles)
    start_row = start_embed[None]
    q_t, k_t, v_t, p_t, o_t, first_t = attention_forward(x_all, start_row, norm_gain, norm_shift, w_t, b_cols, cos, sin)
    cot_moved, _ = lax.optimization_barrier((cot_moved, o_t))
    cot = jnp.where(homes.native, cotangent[0], cot_moved)
    layer_out, gmid, branch, do_t, theirs, mine, small_feed = feed_forward(
        at, o_t, x_all, start_row, norm_gain, norm_shift, w_out, b_out[None], w_up, b_up[None], w_down,
        b_down[None], cot,
    )
    chain = Chain(do_t)
    down = Chunk(theirs[0], swap(theirs[0], "cc"), mine[0])
    up = Chunk(theirs[1], swap(theirs[1], "cc"), mine[1])
    down.halve(chain, "a")
    up.halve(chain, "z")
    gq, gk, gv, gbqkv = chain.then(attention_backward, q_t, k_t, v_t, p_t, o_t, do_t, cos, sin)
    down.halve(chain, "b")
    head_inputs = (gq, gk, gv, first_t, o_t, branch)
    head_theirs = chain.then(lambda *args: heads_first(at, *args), *head_inputs)
    head_received = tuple(swap(piece, "cc") for piece in head_theirs)
    down.quarter(chain)
    head_mine, gx_own, gx_near, gx_core = chain.then(lambda *args: heads_second(at, *args), *head_inputs, w_t)
    heads = Chunk(None, head_received, head_mine)
    gx_core = swap(gx_core, "cc")
    heads.halve(chain, "a")
    gx_near = chain.then(lambda a, b: (a + b[rows:].astype(F32)).astype(BF), gx_near, gx_core)
    gx_near = swap(gx_near, "zz")
    up.halve(chain, "a")
    down_sum = down.finish(chain)
    layer_moved = homes.move(layer_out, None, (1, 2))
    heads.halve(chain, "b")
    up.halve(chain, "b")
    grad_tokens, small_entry = chain.then(
        lambda *args: entry_backward(args[:3], *args[3:]), gx_own, gx_core, gx_near, x_all, start_row, norm_gain, gmid
    )
    tokens_moved = homes.move(grad_tokens, None, (1, 2))
    hidden_bias = [jnp.concatenate([a[2][:, 0], b[2][:, 0]]) for a, b in ((mine, theirs), (theirs, mine))]
    smalls = jnp.concatenate(
        [small_feed, jnp.where(core == 0, hidden_bias[0], hidden_bias[1]), gbqkv[:, 0], small_entry]
    )
    smalls = sum_small(chain, smalls, "dp", [1])
    heads.quarter(chain)
    up.halve(chain, "w")
    smalls = sum_small(chain, smalls, "dp", [2, 4, 6])
    for k in range(3, lax.axis_size("dp").bit_length() - 1):
        smalls = sum_small(chain, smalls, "dp", [1 << k])
    up_sum = up.finish(chain)
    feed = Gather(chain, [down_sum, up_sum])
    heads = Gather(chain, [heads.finish(chain)])
    smalls = sum_small(chain, smalls, "seq", [1, 2, 3])
    feed.double(chain)
    heads.double(chain)
    feed.double(chain)
    heads.double(chain)

    def settled(smalls, layer, tokens):
        gain_1, shift_1, grad_bout, grad_bdown = smalls[:4]
        grad_bqkv = smalls[-6:-3].reshape(3, HEADS, HEAD_DIM).transpose(1, 0, 2).reshape(-1)
        gain_0, shift_0, grad_start = smalls[-3:]
        return (
            jnp.where(homes.native, layer_out, layer)[None],
            jnp.where(homes.native, grad_tokens, tokens)[None],
            grad_start,
            jnp.stack([gain_0, gain_1]),
            jnp.stack([shift_0, shift_1]),
            grad_bqkv,
            grad_bout,
            smalls[4:-6].reshape(-1),
            grad_bdown,
        )

    small_outs = chain.then(settled, smalls, layer_moved, tokens_moved)
    feed.cross(chain)
    (grad_down,) = feed.spread(chain, "down", 0)
    (grad_up,) = feed.spread(chain, "up", 1)
    heads.cross(chain)
    grad_qkv, grad_wout = heads.spread(chain, "heads", 0)
    layer, tokens_grad, grad_start, grad_gain, grad_shift, grad_bqkv, grad_bout, grad_bup, grad_bdown = small_outs
    return (
        layer, tokens_grad, grad_start, grad_gain, grad_shift, grad_qkv, grad_bqkv, grad_wout, grad_bout, grad_up,
        grad_bup, grad_down, grad_bdown,
    )


def solution(mesh):
    rows = P("dp", "seq", None)
    return jax.shard_map(
        per_device,
        mesh=mesh,
        in_specs=(rows, P("dp", "seq"), P("dp")) + (P(),) * 11 + (rows,),
        out_specs=(rows, rows) + (P(),) * 11,
        check_vma=False,
    )
```

```python
import math

import jax
import jax.numpy as jnp
from jax import lax
from jax.experimental import pallas as pl
from jax.experimental.pallas import tpu as pltpu
from jax.sharding import PartitionSpec as P

HEADS = 12
HEAD_DIM = 64
EPS = 1e-05
BF = jnp.bfloat16
F32 = jnp.float32
VMEM_LIMIT = 56 * 1024 * 1024
HEADS_PER_STEP = 4
LIGHT = pl.CostEstimate(flops=1, bytes_accessed=1, transcendentals=0)


def dot(a, b, dims):
    return lax.dot_general(a, b, (dims, ((), ())), preferred_element_type=F32)


NN = ((1,), (0,))
NT = ((1,), (1,))
TN = ((0,), (0,))


def params(**kw):
    return pltpu.CompilerParams(vmem_limit_bytes=VMEM_LIMIT, **kw)


def unit_norm(values):
    centered = values - jnp.mean(values, axis=-1, keepdims=True)
    inverse = lax.rsqrt(jnp.mean(centered * centered, axis=-1, keepdims=True) + EPS)
    return centered * inverse, inverse


def norm_back(grad, unit, inverse, gain):
    e = grad * gain
    inner = e - jnp.mean(e, axis=-1, keepdims=True) - unit * jnp.mean(e * unit, axis=-1, keepdims=True)
    return inner * inverse


def start_flag(x_ref, rows):
    return x_ref[0, rows : rows + 1, 2 * rows : 2 * rows + 1].astype(F32)


def table(ref):
    return jnp.concatenate([ref[i] for i in range(ref.shape[0])], axis=1)


def forward_kernel(
    x_ref, shift_in_ref, gain_ref, shift_ref, w_ref, b_ref, cos_ref, sin_ref,
    q_out, k_out, v_out, p_out, o_out, first_t_out, first_ref,
):
    group = pl.program_id(0)
    rows = q_out.shape[1]

    @pl.when(group == 0)
    def _():
        x = jnp.concatenate([x_ref[i, :rows] for i in range(x_ref.shape[0])], axis=0)
        residual = x.astype(F32) + start_flag(x_ref, rows) * shift_in_ref[...]
        unit, _ = unit_norm(residual)
        first = unit * gain_ref[0:1, :] + shift_ref[0:1, :]
        first_ref[...] = first.astype(BF)
        first_t_out[...] = first.astype(BF).T

    half = HEAD_DIM // 2
    cos, sin = table(cos_ref), table(sin_ref)
    first = first_ref[...]
    query = dot(w_ref[0], first[:rows], NT) + b_ref[0]
    keys = dot(w_ref[1], first, NT) + b_ref[1]
    values = (dot(w_ref[2], first, NT) + b_ref[2]).astype(BF)
    v_out[...] = values

    def rotated(part, head, width):
        lo = part[head * HEAD_DIM : head * HEAD_DIM + half]
        hi = part[head * HEAD_DIM + half : (head + 1) * HEAD_DIM]
        c, s = cos[:, :width], sin[:, :width]
        return jnp.concatenate([lo * c - hi * s, hi * c + lo * s], axis=0)

    for head in range(HEADS_PER_STEP):
        at = slice(head * HEAD_DIM, (head + 1) * HEAD_DIM)
        q_t = (rotated(query, head, rows) * HEAD_DIM**-0.5).astype(BF)
        k_t = rotated(keys, head, first.shape[0])
        q_out[at, :] = q_t
        k_out[at, :] = k_t.astype(BF)
        scores = dot(k_t.T.astype(BF), q_t, NN)
        top = jnp.max(scores, axis=0, keepdims=True)
        weights = jnp.exp(scores - top)
        total = jnp.sum(weights, axis=0, keepdims=True)
        weights = (weights * (1.0 / total)).astype(BF)
        p_out[head] = weights
        o_out[at, :] = dot(values[at], weights, NN)


def attention_forward(x_all, start_row, gain, shift, w_t, b_cols, cos, sin):
    rows, width = cos.shape[2], x_all.shape[2]
    length = cos.shape[0] * rows
    step = HEADS_PER_STEP * HEAD_DIM
    whole = lambda shape: pl.BlockSpec(shape, lambda g: (0,) * len(shape))
    return pl.pallas_call(
        forward_kernel,
        grid=(HEADS // HEADS_PER_STEP,),
        in_specs=[
            whole(x_all.shape),
            whole((1, width)),
            whole((2, width)),
            whole((2, width)),
            pl.BlockSpec((3, step, width), lambda g: (0, g, 0)),
            pl.BlockSpec((3, step, 1), lambda g: (0, g, 0)),
            whole(cos.shape),
            whole(sin.shape),
        ],
        out_specs=[
            pl.BlockSpec((step, rows), lambda g: (g, 0)),
            pl.BlockSpec((step, length), lambda g: (g, 0)),
            pl.BlockSpec((step, length), lambda g: (g, 0)),
            pl.BlockSpec((HEADS_PER_STEP, length, rows), lambda g: (g, 0, 0)),
            pl.BlockSpec((step, rows), lambda g: (g, 0)),
            whole((width, length)),
        ],
        out_shape=[
            jax.ShapeDtypeStruct((width, rows), BF),
            jax.ShapeDtypeStruct((width, length), BF),
            jax.ShapeDtypeStruct((width, length), BF),
            jax.ShapeDtypeStruct((HEADS, length, rows), BF),
            jax.ShapeDtypeStruct((width, rows), F32),
            jax.ShapeDtypeStruct((width, length), BF),
        ],
        scratch_shapes=[pltpu.VMEM((length, width), BF)],
        compiler_params=params(),
        name="attention_forward",
        cost_estimate=LIGHT,
    )(x_all, start_row, gain, shift, w_t, b_cols, cos, sin)


def whole(shape):
    return pl.BlockSpec(shape, lambda *_: (0,) * len(shape))


def feed_chunk(second, second_t, cot, w_up, b_up, w_down):
    hidden = dot(second, w_up, NN) + b_up
    cdf = 0.5 + 0.5 * lax.erf(hidden * (0.5**0.5))
    active = (hidden * cdf).astype(BF)
    slope = cdf + hidden * (jnp.exp(-0.5 * hidden * hidden) * (1.0 / math.sqrt(2.0 * math.pi)))
    out = dot(active, w_down, NN)
    ghid = (dot(cot, w_down, NT) * slope).astype(BF)
    gsec = dot(ghid, w_up, NT)
    gdown = dot(active, cot, TN).astype(BF)
    gup = dot(second_t, ghid, NN).astype(BF)
    return out, gsec, gdown, gup, jnp.sum(ghid.astype(F32), axis=0, keepdims=True)


def store_blocks(out_ref, value, at_ref, base):
    rows = out_ref.shape[2]
    for block in range(8):
        place = block ^ (at_ref[base + 1] * 4 + at_ref[base + 2] * 2 + at_ref[base + 3])
        out_ref[0, place] = value[block * rows : (block + 1) * rows]


def feed_first_kernel(
    at_ref, o_ref, x_ref, start_ref, gain_ref, shift_ref, w_out_ref, b_out_ref, w_up_ref, b_up_ref, w_down_ref, cot_ref,
    middle_ref, second_ref, second_t_ref, acc_ref, gsec_ref, gdown_ref, gup_ref, gbup_ref,
):
    @pl.when(pl.program_id(0) == 0)
    def _():
        attended = o_ref[...].T.astype(BF)
        rows = o_ref.shape[1]
        residual = x_ref[0, :rows].astype(F32) + start_flag(x_ref, rows) * start_ref[...]
        middle = residual + dot(attended, w_out_ref[...], NN) + b_out_ref[...]
        middle_ref[...] = middle
        unit, _ = unit_norm(middle)
        second = unit * gain_ref[1:2, :] + shift_ref[1:2, :]
        second_ref[...] = second.astype(BF)
        second_t_ref[...] = second.T.astype(BF)
        acc_ref[...] = jnp.zeros_like(acc_ref)
        gsec_ref[...] = jnp.zeros_like(gsec_ref)

    out, gsec, gdown, gup, gbup_ref[0] = feed_chunk(
        second_ref[...], second_t_ref[...], cot_ref[...], w_up_ref[...], b_up_ref[...], w_down_ref[...]
    )
    store_blocks(gdown_ref, gdown, at_ref, 5)
    store_blocks(gup_ref, gup, at_ref, 5)
    acc_ref[...] += out
    gsec_ref[...] += gsec


def feed_second_kernel(
    at_ref, middle_ref, second_ref, second_t_ref, acc_in_ref, gsec_in_ref, gain_ref, w_out_ref, w_up_ref, b_up_ref,
    w_down_ref, b_down_ref, cot_ref,
    layer_ref, gmid_ref, branch_ref, do_ref, gdown_ref, gup_ref, gbup_ref, small_ref,
    acc_ref, gsec_ref,
):
    s = pl.program_id(0)

    @pl.when(s == 0)
    def _():
        acc_ref[...] = acc_in_ref[...]
        gsec_ref[...] = gsec_in_ref[...]

    out, gsec, gdown, gup, gbup_ref[0] = feed_chunk(
        second_ref[...], second_t_ref[...], cot_ref[...], w_up_ref[...], b_up_ref[...], w_down_ref[...]
    )
    store_blocks(gdown_ref, gdown, at_ref, 1)
    store_blocks(gup_ref, gup, at_ref, 1)
    acc_ref[...] += out
    gsec_ref[...] += gsec

    @pl.when(s == pl.num_programs(0) - 1)
    def _():
        cot = cot_ref[...].astype(F32)
        middle = middle_ref[...]
        unit, inverse = unit_norm(middle)
        layer_ref[...] = (middle + acc_ref[...] + b_down_ref[...]).astype(BF)
        gsec = gsec_ref[...]
        gmid = cot + norm_back(gsec, unit, inverse, gain_ref[1:2, :])
        gmid_ref[...] = gmid
        branch = gmid.astype(BF)
        branch_ref[...] = branch
        do_ref[...] = dot(w_out_ref[...], branch, NT).astype(BF)
        total = lambda v: jnp.sum(v, axis=0, keepdims=True)
        small_ref[0:1, :] = total(gsec * unit)
        small_ref[1:2, :] = total(gsec)
        small_ref[2:3, :] = total(branch.astype(F32))
        small_ref[3:4, :] = total(cot)


def feed_forward(at, o_t, x_all, start_row, gain, shift, w_out, b_out, w_up, b_up, w_down, b_down, cot):
    rows, width = cot.shape
    steps = w_up.shape[1] // width // 2
    shape = lambda *dims, kind=F32: jax.ShapeDtypeStruct(dims, kind)

    def chunk_specs(theirs):
        chunk = lambda s, at: (steps * jnp.where(theirs, 1 - at[0], at[0]) + s)
        return [
            pl.BlockSpec((width, width), lambda s, at: (0, chunk(s, at))),
            pl.BlockSpec((1, width), lambda s, at: (0, chunk(s, at))),
            pl.BlockSpec((width, width), lambda s, at: (chunk(s, at), 0)),
        ]

    def grad_specs(base):
        block = pl.BlockSpec((1, 8, width // 8, width), lambda s, at: (s ^ at[base], 0, 0, 0))
        return [
            block,
            block,
            pl.BlockSpec((1, 1, width), lambda s, at: (s, 0, 0)),
        ]

    grad_shapes = [shape(steps, 8, width // 8, width, kind=BF)] * 2 + [shape(steps, 1, width)]
    full, turned = whole((rows, width)), whole((width, rows))
    cost = LIGHT
    middle, second, second_t, acc, gsec, *theirs = pl.pallas_call(
        feed_first_kernel,
        grid_spec=pltpu.PrefetchScalarGridSpec(
            num_scalar_prefetch=1,
            grid=(steps,),
            in_specs=[
                turned, whole((1,) + x_all.shape[1:]), whole((1, width)), whole((2, width)), whole((2, width)), whole((width, width)),
                whole((1, width)), *chunk_specs(True), full,
            ],
            out_specs=[full, full, turned, full, full, *grad_specs(5)],
        ),
        out_shape=[
            shape(rows, width), shape(rows, width, kind=BF), shape(width, rows, kind=BF), shape(rows, width),
            shape(rows, width), *grad_shapes,
        ],
        compiler_params=params(),
        name="feed_first",
        cost_estimate=cost,
    )(at, o_t, x_all, start_row, gain, shift, w_out, b_out, w_up, b_up, w_down, cot)
    layer, gmid, branch, do_t, *mine, small = pl.pallas_call(
        feed_second_kernel,
        grid_spec=pltpu.PrefetchScalarGridSpec(
            num_scalar_prefetch=1,
            grid=(steps,),
            in_specs=[
                full, full, turned, full, full, whole((2, width)), whole((width, width)), *chunk_specs(False),
                whole((1, width)), full,
            ],
            out_specs=[full, full, full, turned, *grad_specs(1), whole((4, width))],
            scratch_shapes=[pltpu.VMEM((rows, width), F32), pltpu.VMEM((rows, width), F32)],
        ),
        out_shape=[
            shape(rows, width, kind=BF), shape(rows, width), shape(rows, width, kind=BF), shape(width, rows, kind=BF),
            *grad_shapes, shape(4, width),
        ],
        compiler_params=params(),
        name="feed_second",
        cost_estimate=cost,
    )(at, middle, second, second_t, acc, gsec, gain, w_out, w_up, b_up, w_down, b_down, cot)
    return layer, gmid, branch, do_t, theirs, mine, small


def backward_kernel(
    q_ref, k_ref, v_ref, p_ref, o_ref, do_ref, cos_ref, sin_ref, gq_ref, gk_ref, gv_ref, gb_ref,
):
    rows = q_ref.shape[1]
    half = HEAD_DIM // 2
    cos, sin = table(cos_ref), table(sin_ref)

    def unrotated(part, width):
        lo, hi = part[:half], part[half:]
        c, s = cos[:, :width], sin[:, :width]
        return jnp.concatenate([lo * c + hi * s, hi * c - lo * s], axis=0)

    gqs, gks, gvs = [], [], []
    for head in range(HEADS_PER_STEP):
        at = slice(head * HEAD_DIM, (head + 1) * HEAD_DIM)
        do_t = do_ref[at, :]
        weights = p_ref[head]
        gweights = dot(v_ref[at, :].T, do_t, NN)
        inner = jnp.sum(do_t.astype(F32) * o_ref[at, :], axis=0, keepdims=True)
        gscores = (weights.astype(F32) * (gweights - inner)).astype(BF)
        gq = dot(k_ref[at, :], gscores, NN) * HEAD_DIM**-0.5
        gk = dot(gscores, q_ref[at, :].T, NN)
        gvs.append(dot(weights, do_t.T, NN).astype(BF))
        gqs.append(unrotated(gq, rows).astype(BF))
        gks.append(unrotated(gk.T, gk.shape[0]).astype(BF))
    gq_ref[...] = jnp.concatenate(gqs, axis=0).T
    gk_ref[...] = jnp.concatenate(gks, axis=0).T
    gv_ref[...] = jnp.concatenate(gvs, axis=1)
    ones = jnp.ones((8, gk_ref.shape[0]), BF)
    gb_ref[0] = dot(ones[:, :rows], gq_ref[...], NN)
    gb_ref[1] = dot(ones, gk_ref[...], NN)
    gb_ref[2] = dot(ones, gv_ref[...], NN)


def attention_backward(q_t, k_t, v_t, p_t, o_t, do_t, cos, sin):
    width, rows = q_t.shape
    length = k_t.shape[1]
    step = HEADS_PER_STEP * HEAD_DIM
    narrow, wide = pl.BlockSpec((step, rows), lambda g: (g, 0)), pl.BlockSpec((step, length), lambda g: (g, 0))
    return pl.pallas_call(
        backward_kernel,
        grid=(HEADS // HEADS_PER_STEP,),
        in_specs=[
            narrow, wide, wide, pl.BlockSpec((HEADS_PER_STEP, length, rows), lambda g: (g, 0, 0)), narrow, narrow,
            whole(cos.shape), whole(sin.shape),
        ],
        out_specs=[pl.BlockSpec((n, step), lambda g: (0, g)) for n in (rows, length, length)]
        + [pl.BlockSpec((3, 8, step), lambda g: (0, 0, g))],
        out_shape=[
            jax.ShapeDtypeStruct((rows, width), BF),
            jax.ShapeDtypeStruct((length, width), BF),
            jax.ShapeDtypeStruct((length, width), BF),
            jax.ShapeDtypeStruct((3, 8, width), F32),
        ],
        compiler_params=params(),
        name="attention_backward",
        cost_estimate=LIGHT,
    )(q_t, k_t, v_t, p_t, o_t, do_t, cos, sin)


def head_grads(store, side, base, at_ref, gq_ref, gk_ref, gv_ref, first_t_ref, o_ref, branch_ref):
    rows = gq_ref.shape[0]
    part = first_t_ref.shape[0] // 2
    size = part // 4
    group = at_ref[base] * 2 + at_ref[base + 1]
    mat = at_ref[base + 2] * 2 + at_ref[base + 3]
    at = [pl.ds(pl.multiple_of(side * part + (place ^ group) * size, 32), size) for place in range(4)]
    first_t = jnp.concatenate([first_t_ref[where, :] for where in at], axis=0)
    attended = jnp.concatenate([o_ref[where, :] for where in at], axis=0).astype(BF)
    grads = (
        dot(first_t[:, :rows], gq_ref[...], NN),
        dot(first_t, gk_ref[...], NN),
        dot(first_t, gv_ref[...], NN),
        dot(attended, branch_ref[...], NN),
    )
    for i, grad in enumerate(grads):
        for place in range(4):
            store(place, i ^ mat, grad[place * size : (place + 1) * size].astype(BF))


def heads_first_kernel(at_ref, gq_ref, gk_ref, gv_ref, first_t_ref, o_ref, branch_ref, *outs):
    def store(place, mat, value):
        outs[place // 2][place % 2, mat] = value

    head_grads(store, 1 - at_ref[0], 5, at_ref, gq_ref, gk_ref, gv_ref, first_t_ref, o_ref, branch_ref)


def heads_second_kernel(
    at_ref, gq_ref, gk_ref, gv_ref, first_t_ref, o_ref, branch_ref, w_ref,
    mine_ref, gx_own, gx_near, gx_core, acc_ref,
):
    group = pl.program_id(0)
    rows = gq_ref.shape[0]
    back = dot(gk_ref[...], w_ref[1], NN) + dot(gv_ref[...], w_ref[2], NN)
    own = dot(gq_ref[...], w_ref[0], NN)

    @pl.when(group == 0)
    def _():
        acc_ref[...] = back

    @pl.when(group > 0)
    def _():
        acc_ref[...] += back

    acc_ref[:rows] += own

    def store(place, mat, value):
        mine_ref[place, mat] = value

    head_grads(store, at_ref[0], 1, at_ref, gq_ref, gk_ref, gv_ref, first_t_ref, o_ref, branch_ref)

    @pl.when(group == pl.num_programs(0) - 1)
    def _():
        gx_own[...] = acc_ref[:rows]
        gx_near[...] = acc_ref[rows : 2 * rows]
        gx_core[...] = acc_ref[2 * rows :].astype(BF)


def heads_specs(rows, width, length):
    step = HEADS_PER_STEP * HEAD_DIM
    column = lambda n: pl.BlockSpec((n, step), lambda g, at: (0, g))
    ins = [column(rows), column(length), column(length), whole((width, length)), whole((width, rows)), column(rows)]
    grad = pl.BlockSpec((4, 4, width // 8, step), lambda g, at: (0, 0, 0, g))
    return ins, grad, jax.ShapeDtypeStruct((4, 4, width // 8, width), BF)


def heads_first(at, gq, gk, gv, first_t, o_t, branch):
    rows, width = gq.shape
    ins, _, _ = heads_specs(rows, width, gk.shape[0])
    piece = pl.BlockSpec((2, 4, width // 8, HEADS_PER_STEP * HEAD_DIM), lambda g, at: (0, 0, 0, g))
    return pl.pallas_call(
        heads_first_kernel,
        grid_spec=pltpu.PrefetchScalarGridSpec(
            num_scalar_prefetch=1, grid=(HEADS // HEADS_PER_STEP,), in_specs=ins, out_specs=[piece] * 2
        ),
        out_shape=[jax.ShapeDtypeStruct((2, 4, width // 8, width), BF)] * 2,
        compiler_params=params(),
        name="heads_first",
        cost_estimate=LIGHT,
    )(at, gq, gk, gv, first_t, o_t, branch)


def heads_second(at, gq, gk, gv, first_t, o_t, branch, w_t):
    rows, width = gq.shape
    ins, grad, shape = heads_specs(rows, width, gk.shape[0])
    step = HEADS_PER_STEP * HEAD_DIM
    piece = lambda kind, n: jax.ShapeDtypeStruct((n * rows, width), kind)
    return pl.pallas_call(
        heads_second_kernel,
        grid_spec=pltpu.PrefetchScalarGridSpec(
            num_scalar_prefetch=1,
            grid=(HEADS // HEADS_PER_STEP,),
            in_specs=ins + [pl.BlockSpec((3, step, width), lambda g, at: (0, g, 0))],
            out_specs=[grad, whole((rows, width)), whole((rows, width)), whole((2 * rows, width))],
            scratch_shapes=[pltpu.VMEM((gk.shape[0], width), F32)],
        ),
        out_shape=[shape, piece(F32, 1), piece(F32, 1), piece(BF, 2)],
        compiler_params=params(),
        name="heads_second",
        cost_estimate=pl.CostEstimate(flops=10**10, bytes_accessed=3 * 10**7, transcendentals=0),
    )(at, gq, gk, gv, first_t, o_t, branch, w_t)


def entry_kernel(own_ref, core_ref, near_ref, x_ref, start_ref, gain_ref, gmid_ref, gtok_ref, small_ref):
    rows = own_ref.shape[0]
    grad = own_ref[...] + core_ref[:rows].astype(F32) + near_ref[...].astype(F32)
    flag = start_flag(x_ref, rows)
    unit, inverse = unit_norm(x_ref[0, :rows].astype(F32) + flag * start_ref[...])
    gres = gmid_ref[...] + norm_back(grad, unit, inverse, gain_ref[0:1, :])
    gtok_ref[...] = gres.astype(BF)
    small_ref[0:1, :] = jnp.sum(grad * unit, axis=0, keepdims=True)
    small_ref[1:2, :] = jnp.sum(grad, axis=0, keepdims=True)
    small_ref[2:3, :] = jnp.sum(gres, axis=0, keepdims=True) * flag


def entry_backward(pieces, x_all, start_row, gain, gmid):
    rows, width = gmid.shape
    ins = [*pieces, x_all, start_row, gain, gmid]
    specs = [whole(a.shape) for a in ins]
    specs[len(pieces)] = whole((1,) + x_all.shape[1:])
    return pl.pallas_call(
        entry_kernel,
        grid=(1,),
        in_specs=specs,
        out_specs=[whole((rows, width)), whole((3, width))],
        out_shape=[jax.ShapeDtypeStruct((rows, width), BF), jax.ShapeDtypeStruct((3, width), F32)],
        compiler_params=params(),
        name="entry_backward",
        cost_estimate=LIGHT,
    )(*ins)


BITS = {"c": ("dp", 1), "x": ("dp", 2), "y": ("dp", 4), "z": ("seq", 1), "w": ("seq", 2)}
ORDER = ("xywz", "yxwz")
LEVELS = {"a": "xy", "b": "yx", "w": "ww", "z": "zz"}


def my_bit(name):
    axis, mask = BITS[name]
    return (lax.axis_index(axis) // mask) % 2


def xor_pairs(size, mask):
    return [(i, i ^ mask) for i in range(size)]


def swap(value, names):
    dp, seq = lax.axis_size("dp"), lax.axis_size("seq")
    pairs = []
    for d in range(dp):
        axis, mask = BITS[names[d % 2]]
        for s in range(seq):
            to = (d ^ mask) * seq + s if axis == "dp" else d * seq + (s ^ mask)
            pairs.append((d * seq + s, to))
    return lax.ppermute(value, ("dp", "seq"), pairs)


def swap_seq(value, mask):
    return lax.ppermute(value, "seq", xor_pairs(lax.axis_size("seq"), mask))


def numbers():
    core = my_bit("c")
    first, second = ([my_bit(name) for name in order] for order in ORDER)
    pick = lambda a, b: jnp.where(core == 0, a, b)
    bits = [pick(a, b) for a, b in zip(first, second)] + [pick(b, a) for a, b in zip(first, second)]
    return jnp.stack([core] + bits).astype(jnp.int32)


class Chain:
    def __init__(self, last):
        self.last = last

    def then(self, step, *args):
        args, _ = lax.optimization_barrier((args, self.last))
        self.last = step(*args)
        return self.last


def add_up(parts):
    return sum(p.astype(F32) for p in parts).astype(BF)


class Part:
    def __init__(self, value, bits):
        self.value, self.bits = value, bits

    def take(self, value, sides):
        if isinstance(value, tuple):
            rest = {bit: side for bit, side in sides.items() if bit != self.bits[0]}
            return Part(None, self.bits[1:]).take(value[sides[self.bits[0]]], rest)
        index = tuple(sides[bit] if bit in sides else slice(None) for bit in self.bits)
        return value.reshape((2,) * len(self.bits) + value.shape[-2:])[index]


class Chunk:
    def __init__(self, theirs, received, mine):
        rows, width = mine.shape[-2:]
        blocks = lambda a: a if isinstance(a, tuple) else a.reshape((16, rows, width))
        self.parts = [Part(blocks(mine), "abwz"), Part(blocks(received), "abwz")]
        self.done = {}

    def step(self, chain, choices):
        parts, done = list(self.parts), dict(self.done)

        def sums(*values):
            out = []
            for choice in choices:
                sides = {**done, **choice}
                taken = [
                    part.take(v, {bit: side for bit, side in sides.items() if bit in part.bits})
                    for part, v in zip(parts, values)
                ]
                out.append(add_up(taken))
            return tuple(out)

        return chain.then(sums, *(part.value for part in parts))

    def halve(self, chain, bit):
        (send,) = self.step(chain, [{bit: 1}])
        self.done[bit] = 0
        left = "".join(b for b in "abwz" if b not in self.done)
        self.parts.append(Part(swap(send, LEVELS[bit]), left))

    def quarter(self, chain):
        seq = lax.axis_size("seq")
        sends = self.step(chain, [{"w": k // 2, "z": k % 2} for k in range(1, seq)])
        self.done.update(w=0, z=0)
        left = "".join(b for b in "abwz" if b not in self.done)
        self.parts += [Part(swap_seq(send, k + 1), left) for k, send in enumerate(sends)]

    def finish(self, chain):
        (held,) = self.step(chain, [{}])
        held = held[None]
        dp = lax.axis_size("dp")
        for k in range(3, dp.bit_length() - 1):
            other = lax.ppermute(held, "dp", xor_pairs(dp, 1 << k))
            held = chain.then(lambda a, b: add_up([a, b]), held, other)
        return held


class Gather:
    def __init__(self, chain, shards):
        self.held = shards[0][None] if len(shards) == 1 else chain.then(lambda *a: jnp.stack(a), *shards)
        self.received = [swap_seq(self.held, k) for k in range(1, lax.axis_size("seq"))]
        self.levels = ["a", "b"]

    def double(self, chain):
        self.held = chain.then(lambda *parts: jnp.concatenate(parts, axis=1), self.held, *self.received)
        self.received = [swap(self.held, LEVELS[self.levels.pop()])]
        if not self.levels:
            self.others = [swap(self.held, "cc")]

    def cross(self, chain):
        received, _ = lax.optimization_barrier((self.received[0], chain.last))
        chain.last = received
        self.others.append(swap(received, "cc"))

    def spread(self, chain, kind, i):
        ins = [self.held, self.received[0], *self.others]
        at = numbers()
        return chain.then(lambda *ins: spread(kind, i, at, list(ins)), *ins)


def sum_small(chain, value, axis, masks):
    size = lax.axis_size(axis)
    parts = [lax.ppermute(value, axis, xor_pairs(size, mask)) for mask in masks]
    return chain.then(lambda *parts: sum(parts), value, *parts)


def spread_kernel(kind, at_ref, *refs):
    ins, outs = refs[:4], refs[4:]
    core = at_ref[0]
    for half in range(2):
        side = core if half == 0 else 1 - core
        b3, b2, b1, b0 = (at_ref[1 + 4 * half + i] for i in range(4))
        for top in range(2):
            src = ins[2 * half + top]
            hi = b3 if top == 0 else 1 - b3
            if kind == "heads":
                for i in range(4):
                    outs[2][side, hi, i ^ (b1 * 2 + b0)] = src[0, i].astype(F32)
                continue
            for i in range(2):
                if kind == "down":
                    outs[0][side, hi, 0, i ^ b0] = src[0, i].astype(F32)
                else:
                    width = src.shape[-1]
                    col = pl.multiple_of((side * 2 + hi) * width, width)
                    outs[0][0, i ^ b0, :, pl.ds(col, width)] = src[0, i].astype(F32)
    if kind == "heads":
        w_qkv, w_out, natural = outs
        for side in range(2):
            for hi in range(2):
                w_out[side, hi, 0] = natural[side, hi, 3]
                q, k, v = (natural[side, hi, i] for i in range(3))
                cuts = [slice(h * HEAD_DIM, (h + 1) * HEAD_DIM) for h in range(q.shape[1] // HEAD_DIM)]
                w_qkv[side, hi, 0] = jnp.concatenate([m[:, cut] for cut in cuts for m in (q, k, v)], axis=1)


def spread(kind, which, at, ins):
    n, _, rows, width = ins[0].shape
    scratch, grid = [], (4,)
    if kind == "heads":
        ins = [a.reshape(n, 2, 4, rows, width) for a in ins]
        grid = (2, 2)
        part = width // 2
        spec = lambda base: pl.BlockSpec(
            (None, 1, 4, rows, part), lambda p, c, at: (which, p ^ at[base + 1], 0, 0, c)
        )
        outs = [(2, 2, 2, rows, 3 * width), (2, 2, 2, rows, width)]
        blocks = [pl.BlockSpec((2, 2, 1, rows, o[4] // 2), lambda p, c, at: (0, 0, p, 0, c)) for o in outs]
        scratch = [pltpu.VMEM((2, 2, 4, rows, part), F32)]
    else:
        ins = [a.reshape(n, 4, 2, rows, width) for a in ins]
        low = lambda base, p, at: p ^ (at[base + 1] * 2 + at[base + 2])
        spec = lambda base: pl.BlockSpec((None, 1, 2, rows, width), lambda p, at: (which, low(base, p, at), 0, 0, 0))
        if kind == "down":
            outs = [(2, 2, 4, 2, rows, width)]
            blocks = [pl.BlockSpec((2, 2, 1, 2, rows, width), lambda p, at: (0, 0, p, 0, 0, 0))]
        else:
            outs = [(4, 2, rows, 4 * width)]
            blocks = [pl.BlockSpec((1, 2, rows, 4 * width), lambda p, at: (p, 0, 0, 0))]
    made = pl.pallas_call(
        lambda *refs: spread_kernel(kind, *refs),
        grid_spec=pltpu.PrefetchScalarGridSpec(
            num_scalar_prefetch=1,
            grid=grid,
            in_specs=[spec(1), spec(1), spec(5), spec(5)],
            out_specs=blocks,
            scratch_shapes=scratch,
        ),
        out_shape=[jax.ShapeDtypeStruct(o, F32) for o in outs],
        compiler_params=params(),
        name="spread_" + kind,
        cost_estimate=LIGHT,
    )(at, *ins)
    return [m.reshape(-1, m.shape[-1]) for m in made]


class Homes:
    def __init__(self):
        self.dp, self.seq = lax.axis_size("dp"), lax.axis_size("seq")
        self.native = (lax.axis_index("seq") // 2) % 2 == my_bit("c")

    def pairs(self, native_step, foreign_step):
        out = []
        for d in range(self.dp):
            for z in range(self.seq):
                step = native_step if z // 2 % 2 == d % 2 else foreign_step
                if step is not None:
                    swap_core, mask = step
                    out.append((d * self.seq + z, (d ^ swap_core) * self.seq + (z ^ mask)))
        return out

    def move(self, value, native_step, foreign_step):
        return lax.ppermute(value, ("dp", "seq"), self.pairs(native_step, foreign_step))

    def settle(self, value):
        return jnp.where(self.native, value, self.move(value, None, (1, 2)))

    def gather(self, tokens, positions, flag, meanwhile):
        rows, width = tokens.shape
        digits = jnp.concatenate([positions // 64, positions % 64, flag]).astype(BF)
        extra = jnp.pad(digits, (0, width - digits.shape[0]))
        value = jnp.concatenate([tokens, jnp.broadcast_to(extra, (8, width))])
        far = self.move(value, None, (1, 3))
        near = self.move(value, (0, 1), (1, 2))
        (near, far), meanwhile = lax.optimization_barrier(((near, far), meanwhile))
        two = jnp.stack([jnp.where(self.native, value, near), jnp.where(self.native, near, far)])
        four = jnp.concatenate([two, swap(two, "cc")])
        return four, meanwhile


def per_device(
    tokens, codon_positions, start_flags, start_embed, norm_gain, norm_shift, w_qkv, b_qkv,
    w_out, b_out, w_up, b_up, w_down, b_down, cotangent,
):
    width = tokens.shape[-1]
    core = my_bit("c").astype(jnp.int32)
    at = numbers()
    homes = Homes()
    by_head = w_qkv.reshape(width, HEADS, 3, HEAD_DIM)
    w_t = by_head.transpose(2, 1, 3, 0).reshape(3, width, width)
    b_cols = b_qkv.reshape(HEADS, 3, HEAD_DIM).transpose(1, 0, 2).reshape(3, width, 1)
    rows = tokens.shape[1]
    x_all, (w_t, b_cols) = homes.gather(tokens[0], codon_positions[0], start_flags, (w_t, b_cols))
    cot_moved = homes.move(cotangent[0], None, (1, 2))
    half = HEAD_DIM // 2
    frequency = 10000.0 ** (-2.0 * jnp.arange(half, dtype=F32) / HEAD_DIM)
    digits = x_all[:, rows, : 2 * rows].astype(F32)
    angles = frequency[None, :, None] * (digits[:, :rows] * 64 + digits[:, rows:])[:, None, :]
    cos, sin = jnp.cos(angles), jnp.sin(angles)
    start_row = start_embed[None]
    q_t, k_t, v_t, p_t, o_t, first_t = attention_forward(x_all, start_row, norm_gain, norm_shift, w_t, b_cols, cos, sin)
    cot_moved, _ = lax.optimization_barrier((cot_moved, o_t))
    cot = jnp.where(homes.native, cotangent[0], cot_moved)
    layer_out, gmid, branch, do_t, theirs, mine, small_feed = feed_forward(
        at, o_t, x_all, start_row, norm_gain, norm_shift, w_out, b_out[None], w_up, b_up[None], w_down,
        b_down[None], cot,
    )
    chain = Chain(do_t)
    down = Chunk(theirs[0], swap(theirs[0], "cc"), mine[0])
    up = Chunk(theirs[1], swap(theirs[1], "cc"), mine[1])
    down.halve(chain, "a")
    up.halve(chain, "z")
    gq, gk, gv, gbqkv = chain.then(attention_backward, q_t, k_t, v_t, p_t, o_t, do_t, cos, sin)
    down.halve(chain, "b")
    head_inputs = (gq, gk, gv, first_t, o_t, branch)
    head_theirs = chain.then(lambda *args: heads_first(at, *args), *head_inputs)
    head_received = tuple(swap(piece, "cc") for piece in head_theirs)
    up.halve(chain, "a")
    down.halve(chain, "z")
    layer_moved = homes.move(layer_out, None, (1, 2))
    head_mine, gx_own, gx_near, gx_core = chain.then(lambda *args: heads_second(at, *args), *head_inputs, w_t)
    heads = Chunk(None, head_received, head_mine)
    gx_core = swap(gx_core, "cc")
    heads.halve(chain, "a")
    up.halve(chain, "b")
    gx_near = chain.then(lambda a, b: (a + b[rows:].astype(F32)).astype(BF), gx_near, gx_core)
    gx_near = swap(gx_near, "zz")
    down.halve(chain, "w")
    up.halve(chain, "w")
    heads.halve(chain, "b")
    down_sum = down.finish(chain)
    native = homes.native
    layer_out = chain.then(lambda a, b: jnp.where(native, a, b), layer_out, layer_moved)
    grad_tokens, small_entry = chain.then(
        lambda *args: entry_backward(args[:3], *args[3:]), gx_own, gx_core, gx_near, x_all, start_row, norm_gain, gmid
    )
    hidden_bias = [jnp.concatenate([a[2][:, 0], b[2][:, 0]]) for a, b in ((mine, theirs), (theirs, mine))]
    smalls = jnp.concatenate(
        [small_feed, jnp.where(core == 0, hidden_bias[0], hidden_bias[1]), gbqkv[:, 0], small_entry]
    )
    up_sum = up.finish(chain)
    heads.halve(chain, "z")
    feed = Gather(chain, [down_sum, up_sum])
    smalls = sum_small(chain, smalls, "dp", [1])
    heads.halve(chain, "w")
    for k in range(1, lax.axis_size("dp").bit_length() - 1):
        smalls = sum_small(chain, smalls, "dp", [1 << k])
    feed.double(chain)
    heads = Gather(chain, [heads.finish(chain)])
    smalls = sum_small(chain, smalls, "seq", [1])
    smalls = sum_small(chain, smalls, "seq", [2])
    tokens_moved = homes.move(grad_tokens, None, (1, 2))
    feed.double(chain)
    heads.double(chain)
    grad_tokens = chain.then(lambda a, b: jnp.where(native, a, b), grad_tokens, tokens_moved)

    def settled(smalls):
        gain_1, shift_1, grad_bout, grad_bdown = smalls[:4]
        grad_bqkv = smalls[-6:-3].reshape(3, HEADS, HEAD_DIM).transpose(1, 0, 2).reshape(-1)
        gain_0, shift_0, grad_start = smalls[-3:]
        return (
            grad_start,
            jnp.stack([gain_0, gain_1]),
            jnp.stack([shift_0, shift_1]),
            grad_bqkv,
            grad_bout,
            smalls[4:-6].reshape(-1),
            grad_bdown,
        )

    small_outs = chain.then(settled, smalls)
    heads.double(chain)
    feed.cross(chain)
    (grad_down,) = feed.spread(chain, "down", 0)
    (grad_up,) = feed.spread(chain, "up", 1)
    heads.cross(chain)
    grad_qkv, grad_wout = heads.spread(chain, "heads", 0)
    grad_start, grad_gain, grad_shift, grad_bqkv, grad_bout, grad_bup, grad_bdown = small_outs
    return (
        layer_out[None], grad_tokens[None], grad_start, grad_gain, grad_shift, grad_qkv, grad_bqkv, grad_wout, grad_bout, grad_up,
        grad_bup, grad_down, grad_bdown,
    )


def solution(mesh):
    rows = P("dp", "seq", None)
    return jax.shard_map(
        per_device,
        mesh=mesh,
        in_specs=(rows, P("dp", "seq"), P("dp")) + (P(),) * 11 + (rows,),
        out_specs=(rows, rows) + (P(),) * 11,
        check_vma=False,
    )
```

```python
import math

import jax
import jax.numpy as jnp
from jax import lax
from jax.experimental import pallas as pl
from jax.experimental.pallas import tpu as pltpu
from jax.sharding import PartitionSpec as P

HEADS = 12
HEAD_DIM = 64
EPS = 1e-05
BF = jnp.bfloat16
F32 = jnp.float32
VMEM_LIMIT = 56 * 1024 * 1024
HEADS_PER_STEP = 4
LIGHT = pl.CostEstimate(flops=1, bytes_accessed=1, transcendentals=0)


def dot(a, b, dims):
    return lax.dot_general(a, b, (dims, ((), ())), preferred_element_type=F32)


NN = ((1,), (0,))
NT = ((1,), (1,))
TN = ((0,), (0,))


def params(**kw):
    return pltpu.CompilerParams(vmem_limit_bytes=VMEM_LIMIT, **kw)


def unit_norm(values):
    centered = values - jnp.mean(values, axis=-1, keepdims=True)
    inverse = lax.rsqrt(jnp.mean(centered * centered, axis=-1, keepdims=True) + EPS)
    return centered * inverse, inverse


def norm_back(grad, unit, inverse, gain):
    e = grad * gain
    inner = e - jnp.mean(e, axis=-1, keepdims=True) - unit * jnp.mean(e * unit, axis=-1, keepdims=True)
    return inner * inverse


def start_flag(x_ref, rows):
    return x_ref[0, rows : rows + 1, 2 * rows : 2 * rows + 1].astype(F32)


def table(ref):
    return jnp.concatenate([ref[i] for i in range(ref.shape[0])], axis=1)


def forward_kernel(
    x_ref, shift_in_ref, gain_ref, shift_ref, w_ref, b_ref, cos_ref, sin_ref,
    q_out, k_out, v_out, p_out, o_out, first_t_out, first_ref,
):
    group = pl.program_id(0)
    rows = q_out.shape[1]

    @pl.when(group == 0)
    def _():
        x = jnp.concatenate([x_ref[i, :rows] for i in range(x_ref.shape[0])], axis=0)
        residual = x.astype(F32) + start_flag(x_ref, rows) * shift_in_ref[...]
        unit, _ = unit_norm(residual)
        first = unit * gain_ref[0:1, :] + shift_ref[0:1, :]
        first_ref[...] = first.astype(BF)
        first_t_out[...] = first.astype(BF).T

    half = HEAD_DIM // 2
    cos, sin = table(cos_ref), table(sin_ref)
    first = first_ref[...]
    query = dot(w_ref[0], first[:rows], NT) + b_ref[0]
    keys = dot(w_ref[1], first, NT) + b_ref[1]
    values = (dot(w_ref[2], first, NT) + b_ref[2]).astype(BF)
    v_out[...] = values

    def rotated(part, head, width):
        lo = part[head * HEAD_DIM : head * HEAD_DIM + half]
        hi = part[head * HEAD_DIM + half : (head + 1) * HEAD_DIM]
        c, s = cos[:, :width], sin[:, :width]
        return jnp.concatenate([lo * c - hi * s, hi * c + lo * s], axis=0)

    for head in range(HEADS_PER_STEP):
        at = slice(head * HEAD_DIM, (head + 1) * HEAD_DIM)
        q_t = (rotated(query, head, rows) * HEAD_DIM**-0.5).astype(BF)
        k_t = rotated(keys, head, first.shape[0])
        q_out[at, :] = q_t
        k_t = k_t.astype(BF)
        k_out[at, :] = k_t
        scores = dot(k_t.T, q_t, NN)
        top = jnp.max(scores, axis=0, keepdims=True)
        weights = jnp.exp(scores - top)
        total = jnp.sum(weights, axis=0, keepdims=True)
        weights = (weights * (1.0 / total)).astype(BF)
        p_out[head] = weights
        o_out[at, :] = dot(values[at], weights, NN)


def attention_forward(x_all, start_row, gain, shift, w_t, b_cols, cos, sin):
    rows, width = cos.shape[2], x_all.shape[2]
    length = cos.shape[0] * rows
    step = HEADS_PER_STEP * HEAD_DIM
    whole = lambda shape: pl.BlockSpec(shape, lambda g: (0,) * len(shape))
    return pl.pallas_call(
        forward_kernel,
        grid=(HEADS // HEADS_PER_STEP,),
        in_specs=[
            whole(x_all.shape),
            whole((1, width)),
            whole((2, width)),
            whole((2, width)),
            pl.BlockSpec((3, step, width), lambda g: (0, g, 0)),
            pl.BlockSpec((3, step, 1), lambda g: (0, g, 0)),
            whole(cos.shape),
            whole(sin.shape),
        ],
        out_specs=[
            pl.BlockSpec((step, rows), lambda g: (g, 0)),
            pl.BlockSpec((step, length), lambda g: (g, 0)),
            pl.BlockSpec((step, length), lambda g: (g, 0)),
            pl.BlockSpec((HEADS_PER_STEP, length, rows), lambda g: (g, 0, 0)),
            pl.BlockSpec((step, rows), lambda g: (g, 0)),
            whole((width, length)),
        ],
        out_shape=[
            jax.ShapeDtypeStruct((width, rows), BF),
            jax.ShapeDtypeStruct((width, length), BF),
            jax.ShapeDtypeStruct((width, length), BF),
            jax.ShapeDtypeStruct((HEADS, length, rows), BF),
            jax.ShapeDtypeStruct((width, rows), F32),
            jax.ShapeDtypeStruct((width, length), BF),
        ],
        scratch_shapes=[pltpu.VMEM((length, width), BF)],
        compiler_params=params(),
        name="attention_forward",
        cost_estimate=LIGHT,
    )(x_all, start_row, gain, shift, w_t, b_cols, cos, sin)


def whole(shape):
    return pl.BlockSpec(shape, lambda *_: (0,) * len(shape))


def feed_chunk(second, second_t, cot, w_up, b_up, w_down):
    hidden = dot(second, w_up, NN) + b_up
    cdf = 0.5 + 0.5 * lax.erf(hidden * (0.5**0.5))
    active = (hidden * cdf).astype(BF)
    slope = cdf + hidden * (jnp.exp(-0.5 * hidden * hidden) * (1.0 / math.sqrt(2.0 * math.pi)))
    out = dot(active, w_down, NN)
    ghid = (dot(cot, w_down, NT) * slope).astype(BF)
    gsec = dot(ghid, w_up, NT)
    gdown = dot(active, cot, TN).astype(BF)
    gup = dot(second_t, ghid, NN).astype(BF)
    return out, gsec, gdown, gup, jnp.sum(ghid.astype(F32), axis=0, keepdims=True)


def store_blocks(out_ref, value, at_ref, base):
    rows = out_ref.shape[2]
    for block in range(8):
        place = block ^ (at_ref[base + 1] * 4 + at_ref[base + 2] * 2 + at_ref[base + 3])
        out_ref[0, place] = value[block * rows : (block + 1) * rows]


def feed_first_kernel(
    at_ref, o_ref, x_ref, start_ref, gain_ref, shift_ref, w_out_ref, b_out_ref, w_up_ref, b_up_ref, w_down_ref, cot_ref,
    middle_ref, second_ref, second_t_ref, acc_ref, gsec_ref, gdown_ref, gup_ref, gbup_ref,
):
    @pl.when(pl.program_id(0) == 0)
    def _():
        attended = o_ref[...].astype(BF).T
        rows = o_ref.shape[1]
        residual = x_ref[0, :rows].astype(F32) + start_flag(x_ref, rows) * start_ref[...]
        middle = residual + dot(attended, w_out_ref[...], NN) + b_out_ref[...]
        middle_ref[...] = middle
        unit, _ = unit_norm(middle)
        second = unit * gain_ref[1:2, :] + shift_ref[1:2, :]
        second_ref[...] = second.astype(BF)
        second_t_ref[...] = second.astype(BF).T
        acc_ref[...] = jnp.zeros_like(acc_ref)
        gsec_ref[...] = jnp.zeros_like(gsec_ref)

    out, gsec, gdown, gup, gbup_ref[0] = feed_chunk(
        second_ref[...], second_t_ref[...], cot_ref[...], w_up_ref[...], b_up_ref[...], w_down_ref[...]
    )
    store_blocks(gdown_ref, gdown, at_ref, 5)
    store_blocks(gup_ref, gup, at_ref, 5)
    acc_ref[...] += out
    gsec_ref[...] += gsec


def feed_second_kernel(
    at_ref, middle_ref, second_ref, second_t_ref, acc_in_ref, gsec_in_ref, gain_ref, w_out_ref, w_up_ref, b_up_ref,
    w_down_ref, b_down_ref, cot_ref,
    layer_ref, gmid_ref, branch_ref, do_ref, gdown_ref, gup_ref, gbup_ref, small_ref,
    acc_ref, gsec_ref,
):
    s = pl.program_id(0)

    @pl.when(s == 0)
    def _():
        acc_ref[...] = acc_in_ref[...]
        gsec_ref[...] = gsec_in_ref[...]

    out, gsec, gdown, gup, gbup_ref[0] = feed_chunk(
        second_ref[...], second_t_ref[...], cot_ref[...], w_up_ref[...], b_up_ref[...], w_down_ref[...]
    )
    store_blocks(gdown_ref, gdown, at_ref, 1)
    store_blocks(gup_ref, gup, at_ref, 1)
    acc_ref[...] += out
    gsec_ref[...] += gsec

    @pl.when(s == pl.num_programs(0) - 1)
    def _():
        cot = cot_ref[...].astype(F32)
        middle = middle_ref[...]
        unit, inverse = unit_norm(middle)
        layer_ref[...] = (middle + acc_ref[...] + b_down_ref[...]).astype(BF)
        gsec = gsec_ref[...]
        gmid = cot + norm_back(gsec, unit, inverse, gain_ref[1:2, :])
        gmid_ref[...] = gmid
        branch = gmid.astype(BF)
        branch_ref[...] = branch
        do_ref[...] = dot(w_out_ref[...], branch, NT).astype(BF)
        total = lambda v: jnp.sum(v, axis=0, keepdims=True)
        small_ref[0:1, :] = total(gsec * unit)
        small_ref[1:2, :] = total(gsec)
        small_ref[2:3, :] = total(branch.astype(F32))
        small_ref[3:4, :] = total(cot)


def feed_forward(at, o_t, x_all, start_row, gain, shift, w_out, b_out, w_up, b_up, w_down, b_down, cot):
    rows, width = cot.shape
    steps = w_up.shape[1] // width // 2
    shape = lambda *dims, kind=F32: jax.ShapeDtypeStruct(dims, kind)

    def chunk_specs(theirs):
        chunk = lambda s, at: (steps * jnp.where(theirs, 1 - at[0], at[0]) + s)
        return [
            pl.BlockSpec((width, width), lambda s, at: (0, chunk(s, at))),
            pl.BlockSpec((1, width), lambda s, at: (0, chunk(s, at))),
            pl.BlockSpec((width, width), lambda s, at: (chunk(s, at), 0)),
        ]

    def grad_specs(base):
        block = pl.BlockSpec((1, 8, width // 8, width), lambda s, at: (s ^ at[base], 0, 0, 0))
        return [
            block,
            block,
            pl.BlockSpec((1, 1, width), lambda s, at: (s, 0, 0)),
        ]

    grad_shapes = [shape(steps, 8, width // 8, width, kind=BF)] * 2 + [shape(steps, 1, width)]
    full, turned = whole((rows, width)), whole((width, rows))
    cost = LIGHT
    middle, second, second_t, acc, gsec, *theirs = pl.pallas_call(
        feed_first_kernel,
        grid_spec=pltpu.PrefetchScalarGridSpec(
            num_scalar_prefetch=1,
            grid=(steps,),
            in_specs=[
                turned, whole((1,) + x_all.shape[1:]), whole((1, width)), whole((2, width)), whole((2, width)), whole((width, width)),
                whole((1, width)), *chunk_specs(True), full,
            ],
            out_specs=[full, full, turned, full, full, *grad_specs(5)],
        ),
        out_shape=[
            shape(rows, width), shape(rows, width, kind=BF), shape(width, rows, kind=BF), shape(rows, width),
            shape(rows, width), *grad_shapes,
        ],
        compiler_params=params(),
        name="feed_first",
        cost_estimate=cost,
    )(at, o_t, x_all, start_row, gain, shift, w_out, b_out, w_up, b_up, w_down, cot)
    layer, gmid, branch, do_t, *mine, small = pl.pallas_call(
        feed_second_kernel,
        grid_spec=pltpu.PrefetchScalarGridSpec(
            num_scalar_prefetch=1,
            grid=(steps,),
            in_specs=[
                full, full, turned, full, full, whole((2, width)), whole((width, width)), *chunk_specs(False),
                whole((1, width)), full,
            ],
            out_specs=[full, full, full, turned, *grad_specs(1), whole((4, width))],
            scratch_shapes=[pltpu.VMEM((rows, width), F32), pltpu.VMEM((rows, width), F32)],
        ),
        out_shape=[
            shape(rows, width, kind=BF), shape(rows, width), shape(rows, width, kind=BF), shape(width, rows, kind=BF),
            *grad_shapes, shape(4, width),
        ],
        compiler_params=params(),
        name="feed_second",
        cost_estimate=cost,
    )(at, middle, second, second_t, acc, gsec, gain, w_out, w_up, b_up, w_down, b_down, cot)
    return layer, gmid, branch, do_t, theirs, mine, small


def backward_kernel(
    q_ref, k_ref, v_ref, p_ref, o_ref, do_ref, cos_ref, sin_ref, gq_ref, gk_ref, gv_ref, gb_ref,
):
    rows = q_ref.shape[1]
    half = HEAD_DIM // 2
    cos, sin = table(cos_ref), table(sin_ref)

    def unrotated(part, width):
        lo, hi = part[:half], part[half:]
        c, s = cos[:, :width], sin[:, :width]
        return jnp.concatenate([lo * c + hi * s, hi * c - lo * s], axis=0)

    gqs, gks, gvs = [], [], []
    for head in range(HEADS_PER_STEP):
        at = slice(head * HEAD_DIM, (head + 1) * HEAD_DIM)
        do_t = do_ref[at, :]
        weights = p_ref[head]
        gweights = dot(v_ref[at, :].T, do_t, NN)
        inner = jnp.sum(do_t.astype(F32) * o_ref[at, :], axis=0, keepdims=True)
        gscores = (weights.astype(F32) * (gweights - inner)).astype(BF)
        gq = dot(k_ref[at, :], gscores, NN) * HEAD_DIM**-0.5
        gk = dot(gscores, q_ref[at, :].T, NN)
        gvs.append(dot(weights, do_t.T, NN).astype(BF))
        gqs.append(unrotated(gq, rows).astype(BF))
        gks.append(unrotated(gk.T, gk.shape[0]).astype(BF))
    gq_ref[...] = jnp.concatenate(gqs, axis=0).T
    gk_ref[...] = jnp.concatenate(gks, axis=0).T
    gv_ref[...] = jnp.concatenate(gvs, axis=1)
    ones = jnp.ones((8, gk_ref.shape[0]), BF)
    gb_ref[0] = dot(ones[:, :rows], gq_ref[...], NN)
    gb_ref[1] = dot(ones, gk_ref[...], NN)
    gb_ref[2] = dot(ones, gv_ref[...], NN)


def attention_backward(q_t, k_t, v_t, p_t, o_t, do_t, cos, sin):
    width, rows = q_t.shape
    length = k_t.shape[1]
    step = HEADS_PER_STEP * HEAD_DIM
    narrow, wide = pl.BlockSpec((step, rows), lambda g: (g, 0)), pl.BlockSpec((step, length), lambda g: (g, 0))
    return pl.pallas_call(
        backward_kernel,
        grid=(HEADS // HEADS_PER_STEP,),
        in_specs=[
            narrow, wide, wide, pl.BlockSpec((HEADS_PER_STEP, length, rows), lambda g: (g, 0, 0)), narrow, narrow,
            whole(cos.shape), whole(sin.shape),
        ],
        out_specs=[pl.BlockSpec((n, step), lambda g: (0, g)) for n in (rows, length, length)]
        + [pl.BlockSpec((3, 8, step), lambda g: (0, 0, g))],
        out_shape=[
            jax.ShapeDtypeStruct((rows, width), BF),
            jax.ShapeDtypeStruct((length, width), BF),
            jax.ShapeDtypeStruct((length, width), BF),
            jax.ShapeDtypeStruct((3, 8, width), F32),
        ],
        compiler_params=params(),
        name="attention_backward",
        cost_estimate=LIGHT,
    )(q_t, k_t, v_t, p_t, o_t, do_t, cos, sin)


def head_grads(store, side, base, at_ref, gq_ref, gk_ref, gv_ref, first_t_ref, o_ref, branch_ref):
    rows = gq_ref.shape[0]
    part = first_t_ref.shape[0] // 2
    size = part // 4
    group = at_ref[base] * 2 + at_ref[base + 1]
    mat = at_ref[base + 2] * 2 + at_ref[base + 3]
    at = [pl.ds(pl.multiple_of(side * part + (place ^ group) * size, 32), size) for place in range(4)]
    first_t = jnp.concatenate([first_t_ref[where, :] for where in at], axis=0)
    attended = jnp.concatenate([o_ref[where, :] for where in at], axis=0).astype(BF)
    grads = (
        dot(first_t[:, :rows], gq_ref[...], NN),
        dot(first_t, gk_ref[...], NN),
        dot(first_t, gv_ref[...], NN),
        dot(attended, branch_ref[...], NN),
    )
    for i, grad in enumerate(grads):
        for place in range(4):
            store(place, i ^ mat, grad[place * size : (place + 1) * size].astype(BF))


def heads_first_kernel(at_ref, gq_ref, gk_ref, gv_ref, first_t_ref, o_ref, branch_ref, *outs):
    def store(place, mat, value):
        outs[place // 2][place % 2, mat] = value

    head_grads(store, 1 - at_ref[0], 5, at_ref, gq_ref, gk_ref, gv_ref, first_t_ref, o_ref, branch_ref)


def heads_second_kernel(
    at_ref, gq_ref, gk_ref, gv_ref, first_t_ref, o_ref, branch_ref, w_ref,
    mine_ref, gx_own, gx_near, gx_core, acc_ref,
):
    group = pl.program_id(0)
    rows = gq_ref.shape[0]
    back = dot(gk_ref[...], w_ref[1], NN) + dot(gv_ref[...], w_ref[2], NN)
    own = dot(gq_ref[...], w_ref[0], NN)

    @pl.when(group == 0)
    def _():
        acc_ref[...] = back

    @pl.when(group > 0)
    def _():
        acc_ref[...] += back

    acc_ref[:rows] += own

    def store(place, mat, value):
        mine_ref[place, mat] = value

    head_grads(store, at_ref[0], 1, at_ref, gq_ref, gk_ref, gv_ref, first_t_ref, o_ref, branch_ref)

    @pl.when(group == pl.num_programs(0) - 1)
    def _():
        gx_own[...] = acc_ref[:rows]
        gx_near[...] = acc_ref[rows : 2 * rows]
        gx_core[...] = acc_ref[2 * rows :].astype(BF)


def heads_specs(rows, width, length):
    step = HEADS_PER_STEP * HEAD_DIM
    column = lambda n: pl.BlockSpec((n, step), lambda g, at: (0, g))
    ins = [column(rows), column(length), column(length), whole((width, length)), whole((width, rows)), column(rows)]
    grad = pl.BlockSpec((4, 4, width // 8, step), lambda g, at: (0, 0, 0, g))
    return ins, grad, jax.ShapeDtypeStruct((4, 4, width // 8, width), BF)


def heads_first(at, gq, gk, gv, first_t, o_t, branch):
    rows, width = gq.shape
    ins, _, _ = heads_specs(rows, width, gk.shape[0])
    piece = pl.BlockSpec((2, 4, width // 8, HEADS_PER_STEP * HEAD_DIM), lambda g, at: (0, 0, 0, g))
    return pl.pallas_call(
        heads_first_kernel,
        grid_spec=pltpu.PrefetchScalarGridSpec(
            num_scalar_prefetch=1, grid=(HEADS // HEADS_PER_STEP,), in_specs=ins, out_specs=[piece] * 2
        ),
        out_shape=[jax.ShapeDtypeStruct((2, 4, width // 8, width), BF)] * 2,
        compiler_params=params(),
        name="heads_first",
        cost_estimate=LIGHT,
    )(at, gq, gk, gv, first_t, o_t, branch)


def heads_second(at, gq, gk, gv, first_t, o_t, branch, w_t):
    rows, width = gq.shape
    ins, grad, shape = heads_specs(rows, width, gk.shape[0])
    step = HEADS_PER_STEP * HEAD_DIM
    piece = lambda kind, n: jax.ShapeDtypeStruct((n * rows, width), kind)
    return pl.pallas_call(
        heads_second_kernel,
        grid_spec=pltpu.PrefetchScalarGridSpec(
            num_scalar_prefetch=1,
            grid=(HEADS // HEADS_PER_STEP,),
            in_specs=ins + [pl.BlockSpec((3, step, width), lambda g, at: (0, g, 0))],
            out_specs=[grad, whole((rows, width)), whole((rows, width)), whole((2 * rows, width))],
            scratch_shapes=[pltpu.VMEM((gk.shape[0], width), F32)],
        ),
        out_shape=[shape, piece(F32, 1), piece(F32, 1), piece(BF, 2)],
        compiler_params=params(),
        name="heads_second",
        cost_estimate=pl.CostEstimate(flops=10**10, bytes_accessed=3 * 10**7, transcendentals=0),
    )(at, gq, gk, gv, first_t, o_t, branch, w_t)


def entry_kernel(own_ref, core_ref, near_ref, x_ref, start_ref, gain_ref, gmid_ref, gtok_ref, small_ref):
    rows = own_ref.shape[0]
    grad = own_ref[...] + core_ref[:rows].astype(F32) + near_ref[...].astype(F32)
    flag = start_flag(x_ref, rows)
    unit, inverse = unit_norm(x_ref[0, :rows].astype(F32) + flag * start_ref[...])
    gres = gmid_ref[...] + norm_back(grad, unit, inverse, gain_ref[0:1, :])
    gtok_ref[...] = gres.astype(BF)
    small_ref[0:1, :] = jnp.sum(grad * unit, axis=0, keepdims=True)
    small_ref[1:2, :] = jnp.sum(grad, axis=0, keepdims=True)
    small_ref[2:3, :] = jnp.sum(gres, axis=0, keepdims=True) * flag


def entry_backward(pieces, x_all, start_row, gain, gmid):
    rows, width = gmid.shape
    ins = [*pieces, x_all, start_row, gain, gmid]
    specs = [whole(a.shape) for a in ins]
    specs[len(pieces)] = whole((1,) + x_all.shape[1:])
    return pl.pallas_call(
        entry_kernel,
        grid=(1,),
        in_specs=specs,
        out_specs=[whole((rows, width)), whole((3, width))],
        out_shape=[jax.ShapeDtypeStruct((rows, width), BF), jax.ShapeDtypeStruct((3, width), F32)],
        compiler_params=params(),
        name="entry_backward",
        cost_estimate=LIGHT,
    )(*ins)


BITS = {"c": ("dp", 1), "x": ("dp", 2), "y": ("dp", 4), "z": ("seq", 1), "w": ("seq", 2)}
ORDER = ("xywz", "yxwz")
LEVELS = {"a": "xy", "b": "yx", "w": "ww", "z": "zz"}


def my_bit(name):
    axis, mask = BITS[name]
    return (lax.axis_index(axis) // mask) % 2


def xor_pairs(size, mask):
    return [(i, i ^ mask) for i in range(size)]


def swap(value, names):
    dp, seq = lax.axis_size("dp"), lax.axis_size("seq")
    pairs = []
    for d in range(dp):
        axis, mask = BITS[names[d % 2]]
        for s in range(seq):
            to = (d ^ mask) * seq + s if axis == "dp" else d * seq + (s ^ mask)
            pairs.append((d * seq + s, to))
    return lax.ppermute(value, ("dp", "seq"), pairs)


def swap_seq(value, mask):
    return lax.ppermute(value, "seq", xor_pairs(lax.axis_size("seq"), mask))


def numbers():
    core = my_bit("c")
    first, second = ([my_bit(name) for name in order] for order in ORDER)
    pick = lambda a, b: jnp.where(core == 0, a, b)
    bits = [pick(a, b) for a, b in zip(first, second)] + [pick(b, a) for a, b in zip(first, second)]
    return jnp.stack([core] + bits).astype(jnp.int32)


class Chain:
    def __init__(self, last):
        self.last = last

    def then(self, step, *args):
        args, _ = lax.optimization_barrier((args, self.last))
        self.last = step(*args)
        return self.last


def add_up(parts):
    return sum(p.astype(F32) for p in parts).astype(BF)


class Part:
    def __init__(self, value, bits):
        self.value, self.bits = value, bits

    def take(self, value, sides):
        if isinstance(value, tuple):
            rest = {bit: side for bit, side in sides.items() if bit != self.bits[0]}
            return Part(None, self.bits[1:]).take(value[sides[self.bits[0]]], rest)
        index = tuple(sides[bit] if bit in sides else slice(None) for bit in self.bits)
        return value.reshape((2,) * len(self.bits) + value.shape[-2:])[index]


class Chunk:
    def __init__(self, theirs, received, mine):
        rows, width = mine.shape[-2:]
        blocks = lambda a: a if isinstance(a, tuple) else a.reshape((16, rows, width))
        self.parts = [Part(blocks(mine), "abwz"), Part(blocks(received), "abwz")]
        self.done = {}

    def step(self, chain, choices):
        parts, done = list(self.parts), dict(self.done)

        def sums(*values):
            out = []
            for choice in choices:
                sides = {**done, **choice}
                taken = [
                    part.take(v, {bit: side for bit, side in sides.items() if bit in part.bits})
                    for part, v in zip(parts, values)
                ]
                out.append(add_up(taken))
            return tuple(out)

        return chain.then(sums, *(part.value for part in parts))

    def halve(self, chain, bit):
        (send,) = self.step(chain, [{bit: 1}])
        self.done[bit] = 0
        left = "".join(b for b in "abwz" if b not in self.done)
        self.parts.append(Part(swap(send, LEVELS[bit]), left))

    def quarter(self, chain):
        seq = lax.axis_size("seq")
        sends = self.step(chain, [{"w": k // 2, "z": k % 2} for k in range(1, seq)])
        self.done.update(w=0, z=0)
        left = "".join(b for b in "abwz" if b not in self.done)
        self.parts += [Part(swap_seq(send, k + 1), left) for k, send in enumerate(sends)]

    def finish(self, chain):
        (held,) = self.step(chain, [{}])
        held = held[None]
        dp = lax.axis_size("dp")
        for k in range(3, dp.bit_length() - 1):
            other = lax.ppermute(held, "dp", xor_pairs(dp, 1 << k))
            held = chain.then(lambda a, b: add_up([a, b]), held, other)
        return held


class Gather:
    def __init__(self, chain, shards):
        self.held = shards[0][None] if len(shards) == 1 else chain.then(lambda *a: jnp.stack(a), *shards)
        self.received = [swap_seq(self.held, k) for k in range(1, lax.axis_size("seq"))]
        self.levels = ["a", "b"]

    def double(self, chain):
        self.held = chain.then(lambda *parts: jnp.concatenate(parts, axis=1), self.held, *self.received)
        self.received = [swap(self.held, LEVELS[self.levels.pop()])]
        if not self.levels:
            self.others = [swap(self.held, "cc")]

    def cross(self, chain):
        received, _ = lax.optimization_barrier((self.received[0], chain.last))
        chain.last = received
        self.others.append(swap(received, "cc"))

    def spread(self, chain, kind, i):
        ins = [self.held, self.received[0], *self.others]
        at = numbers()
        return chain.then(lambda *ins: spread(kind, i, at, list(ins)), *ins)


def sum_small(chain, value, axis, masks):
    size = lax.axis_size(axis)
    parts = [lax.ppermute(value, axis, xor_pairs(size, mask)) for mask in masks]
    return chain.then(lambda *parts: sum(parts), value, *parts)


def spread_kernel(kind, at_ref, *refs):
    ins, outs = refs[:4], refs[4:]
    core = at_ref[0]
    for half in range(2):
        side = core if half == 0 else 1 - core
        b3, b2, b1, b0 = (at_ref[1 + 4 * half + i] for i in range(4))
        for top in range(2):
            src = ins[2 * half + top]
            hi = b3 if top == 0 else 1 - b3
            if kind == "heads":
                for i in range(4):
                    outs[2][side, hi, i ^ (b1 * 2 + b0)] = src[0, i].astype(F32)
                continue
            for i in range(2):
                if kind == "down":
                    outs[0][side, hi, 0, i ^ b0] = src[0, i].astype(F32)
                else:
                    width = src.shape[-1]
                    col = pl.multiple_of((side * 2 + hi) * width, width)
                    outs[0][0, i ^ b0, :, pl.ds(col, width)] = src[0, i].astype(F32)
    if kind == "heads":
        w_qkv, w_out, natural = outs
        for side in range(2):
            for hi in range(2):
                w_out[side, hi, 0] = natural[side, hi, 3]
                q, k, v = (natural[side, hi, i] for i in range(3))
                cuts = [slice(h * HEAD_DIM, (h + 1) * HEAD_DIM) for h in range(q.shape[1] // HEAD_DIM)]
                w_qkv[side, hi, 0] = jnp.concatenate([m[:, cut] for cut in cuts for m in (q, k, v)], axis=1)


def spread(kind, which, at, ins):
    n, _, rows, width = ins[0].shape
    scratch, grid = [], (4,)
    if kind == "heads":
        ins = [a.reshape(n, 2, 4, rows, width) for a in ins]
        grid = (2, 2)
        part = width // 2
        spec = lambda base: pl.BlockSpec(
            (None, 1, 4, rows, part), lambda p, c, at: (which, p ^ at[base + 1], 0, 0, c)
        )
        outs = [(2, 2, 2, rows, 3 * width), (2, 2, 2, rows, width)]
        blocks = [pl.BlockSpec((2, 2, 1, rows, o[4] // 2), lambda p, c, at: (0, 0, p, 0, c)) for o in outs]
        scratch = [pltpu.VMEM((2, 2, 4, rows, part), F32)]
    else:
        ins = [a.reshape(n, 4, 2, rows, width) for a in ins]
        low = lambda base, p, at: p ^ (at[base + 1] * 2 + at[base + 2])
        spec = lambda base: pl.BlockSpec((None, 1, 2, rows, width), lambda p, at: (which, low(base, p, at), 0, 0, 0))
        if kind == "down":
            outs = [(2, 2, 4, 2, rows, width)]
            blocks = [pl.BlockSpec((2, 2, 1, 2, rows, width), lambda p, at: (0, 0, p, 0, 0, 0))]
        else:
            outs = [(4, 2, rows, 4 * width)]
            blocks = [pl.BlockSpec((1, 2, rows, 4 * width), lambda p, at: (p, 0, 0, 0))]
    made = pl.pallas_call(
        lambda *refs: spread_kernel(kind, *refs),
        grid_spec=pltpu.PrefetchScalarGridSpec(
            num_scalar_prefetch=1,
            grid=grid,
            in_specs=[spec(1), spec(1), spec(5), spec(5)],
            out_specs=blocks,
            scratch_shapes=scratch,
        ),
        out_shape=[jax.ShapeDtypeStruct(o, F32) for o in outs],
        compiler_params=params(),
        name="spread_" + kind,
        cost_estimate=LIGHT,
    )(at, *ins)
    return [m.reshape(-1, m.shape[-1]) for m in made]


class Homes:
    def __init__(self):
        self.dp, self.seq = lax.axis_size("dp"), lax.axis_size("seq")
        self.native = (lax.axis_index("seq") // 2) % 2 == my_bit("c")

    def pairs(self, native_step, foreign_step):
        out = []
        for d in range(self.dp):
            for z in range(self.seq):
                step = native_step if z // 2 % 2 == d % 2 else foreign_step
                if step is not None:
                    swap_core, mask = step
                    out.append((d * self.seq + z, (d ^ swap_core) * self.seq + (z ^ mask)))
        return out

    def move(self, value, native_step, foreign_step):
        return lax.ppermute(value, ("dp", "seq"), self.pairs(native_step, foreign_step))

    def settle(self, value):
        return jnp.where(self.native, value, self.move(value, None, (1, 2)))

    def gather(self, tokens, positions, flag, meanwhile):
        rows, width = tokens.shape
        digits = jnp.concatenate([positions // 64, positions % 64, flag]).astype(BF)
        extra = jnp.pad(digits, (0, width - digits.shape[0]))
        value = jnp.concatenate([tokens, jnp.broadcast_to(extra, (8, width))])
        far = self.move(value, None, (1, 3))
        near = self.move(value, (0, 1), (1, 2))
        (near, far), meanwhile = lax.optimization_barrier(((near, far), meanwhile))
        two = jnp.stack([jnp.where(self.native, value, near), jnp.where(self.native, near, far)])
        four = jnp.concatenate([two, swap(two, "cc")])
        return four, meanwhile


def per_device(
    tokens, codon_positions, start_flags, start_embed, norm_gain, norm_shift, w_qkv, b_qkv,
    w_out, b_out, w_up, b_up, w_down, b_down, cotangent,
):
    width = tokens.shape[-1]
    core = my_bit("c").astype(jnp.int32)
    at = numbers()
    homes = Homes()
    by_head = w_qkv.reshape(width, HEADS, 3, HEAD_DIM)
    w_t = by_head.transpose(2, 1, 3, 0).reshape(3, width, width)
    b_cols = b_qkv.reshape(HEADS, 3, HEAD_DIM).transpose(1, 0, 2).reshape(3, width, 1)
    rows = tokens.shape[1]
    x_all, (w_t, b_cols) = homes.gather(tokens[0], codon_positions[0], start_flags, (w_t, b_cols))
    cot_moved = homes.move(cotangent[0], None, (1, 2))
    half = HEAD_DIM // 2
    frequency = 10000.0 ** (-2.0 * jnp.arange(half, dtype=F32) / HEAD_DIM)
    digits = x_all[:, rows, : 2 * rows].astype(F32)
    angles = frequency[None, :, None] * (digits[:, :rows] * 64 + digits[:, rows:])[:, None, :]
    cos, sin = jnp.cos(angles), jnp.sin(angles)
    start_row = start_embed[None]
    q_t, k_t, v_t, p_t, o_t, first_t = attention_forward(x_all, start_row, norm_gain, norm_shift, w_t, b_cols, cos, sin)
    cot_moved, _ = lax.optimization_barrier((cot_moved, o_t))
    cot = jnp.where(homes.native, cotangent[0], cot_moved)
    layer_out, gmid, branch, do_t, theirs, mine, small_feed = feed_forward(
        at, o_t, x_all, start_row, norm_gain, norm_shift, w_out, b_out[None], w_up, b_up[None], w_down,
        b_down[None], cot,
    )
    chain = Chain(do_t)
    down = Chunk(theirs[0], swap(theirs[0], "cc"), mine[0])
    up = Chunk(theirs[1], swap(theirs[1], "cc"), mine[1])
    down.halve(chain, "a")
    up.halve(chain, "z")
    gq, gk, gv, gbqkv = chain.then(attention_backward, q_t, k_t, v_t, p_t, o_t, do_t, cos, sin)
    down.halve(chain, "b")
    head_inputs = (gq, gk, gv, first_t, o_t, branch)
    head_theirs = chain.then(lambda *args: heads_first(at, *args), *head_inputs)
    head_received = tuple(swap(piece, "cc") for piece in head_theirs)
    up.halve(chain, "a")
    down.halve(chain, "z")
    layer_moved = homes.move(layer_out, None, (1, 2))
    head_mine, gx_own, gx_near, gx_core = chain.then(lambda *args: heads_second(at, *args), *head_inputs, w_t)
    heads = Chunk(None, head_received, head_mine)
    gx_core = swap(gx_core, "cc")
    heads.halve(chain, "a")
    up.halve(chain, "b")
    gx_near = chain.then(lambda a, b: (a + b[rows:].astype(F32)).astype(BF), gx_near, gx_core)
    gx_near = swap(gx_near, "zz")
    down.halve(chain, "w")
    up.halve(chain, "w")
    heads.halve(chain, "b")
    down_sum = down.finish(chain)
    native = homes.native
    layer_out = chain.then(lambda a, b: jnp.where(native, a, b), layer_out, layer_moved)
    grad_tokens, small_entry = chain.then(
        lambda *args: entry_backward(args[:3], *args[3:]), gx_own, gx_core, gx_near, x_all, start_row, norm_gain, gmid
    )
    hidden_bias = [jnp.concatenate([a[2][:, 0], b[2][:, 0]]) for a, b in ((mine, theirs), (theirs, mine))]
    smalls = jnp.concatenate(
        [small_feed, jnp.where(core == 0, hidden_bias[0], hidden_bias[1]), gbqkv[:, 0], small_entry]
    )
    up_sum = up.finish(chain)
    heads.halve(chain, "z")
    feed = Gather(chain, [down_sum, up_sum])
    smalls = sum_small(chain, smalls, "dp", [1])
    heads.halve(chain, "w")
    for k in range(1, lax.axis_size("dp").bit_length() - 1):
        smalls = sum_small(chain, smalls, "dp", [1 << k])
    feed.double(chain)
    heads = Gather(chain, [heads.finish(chain)])
    smalls = sum_small(chain, smalls, "seq", [1])
    smalls = sum_small(chain, smalls, "seq", [2])
    tokens_moved = homes.move(grad_tokens, None, (1, 2))
    feed.double(chain)
    heads.double(chain)

    def settled(smalls):
        gain_1, shift_1, grad_bout, grad_bdown = smalls[:4]
        grad_bqkv = smalls[-6:-3].reshape(3, HEADS, HEAD_DIM).transpose(1, 0, 2).reshape(-1)
        gain_0, shift_0, grad_start = smalls[-3:]
        return (
            grad_start,
            jnp.stack([gain_0, gain_1]),
            jnp.stack([shift_0, shift_1]),
            grad_bqkv,
            grad_bout,
            smalls[4:-6].reshape(-1),
            grad_bdown,
        )

    small_outs = chain.then(settled, smalls)
    grad_tokens = chain.then(lambda a, b: jnp.where(native, a, b), grad_tokens, tokens_moved)
    heads.double(chain)
    feed.cross(chain)
    (grad_down,) = feed.spread(chain, "down", 0)
    (grad_up,) = feed.spread(chain, "up", 1)
    heads.cross(chain)
    grad_qkv, grad_wout = heads.spread(chain, "heads", 0)
    grad_start, grad_gain, grad_shift, grad_bqkv, grad_bout, grad_bup, grad_bdown = small_outs
    return (
        layer_out[None], grad_tokens[None], grad_start, grad_gain, grad_shift, grad_qkv, grad_bqkv, grad_wout, grad_bout, grad_up,
        grad_bup, grad_down, grad_bdown,
    )


def solution(mesh):
    rows = P("dp", "seq", None)
    return jax.shard_map(
        per_device,
        mesh=mesh,
        in_specs=(rows, P("dp", "seq"), P("dp")) + (P(),) * 11 + (rows,),
        out_specs=(rows, rows) + (P(),) * 11,
        check_vma=False,
    )
```
